32 devices in a mesh: dp: 8 (over z, core), tensor: 4 (over y, x).
Axes of the slice: x: 2, y: 2, z: 4, core: 2. Of those that a mesh axis runs over, the one named last changes fastest.
Arguments:
- hidden_in: bfloat16 [16384, 2048], P(('dp', 'tensor')), may hold values from -6 to 6
- grad_out: bfloat16 [16384, 2048], P(('dp', 'tensor')), may hold values from -6 to 6
- lengths: int32 [16], replicated, may hold values from 256 to 1792, as said below
- owners: int32 [16], replicated, may hold values from 0 to 7, as said below
- qkv_weight: float32 [3, 2048, 2048], P(None, 'dp', 'tensor'), may hold values from -0.125 to 0.125
- out_weight: float32 [2048, 2048], P('tensor', 'dp'), may hold values from -0.5 to 0.5
- gate_up_weight: float32 [2, 2048, 5632], P(None, 'dp', 'tensor'), may hold values from -0.125 to 0.125
- down_weight: float32 [5632, 2048], P('tensor', 'dp'), may hold values from -0.078125 to 0.078125
- norm_gain: float32 [2, 2048], replicated, may hold values from 0.5 to 1.5
- norm_bias: float32 [2, 2048], replicated, may hold values from -1 to 1
- qkv_bias: float32 [3, 2048], replicated, may hold values from -1.5 to 1.5
- qkv_first: float32 [3, 2048, 2048], P(None, 'dp', 'tensor'), may hold values from -8.96 to 8.96
- out_first: float32 [2048, 2048], P('tensor', 'dp'), may hold values from -12.8 to 12.8
- gate_up_first: float32 [2, 2048, 5632], P(None, 'dp', 'tensor'), may hold values from -21.76 to 21.76
- down_first: float32 [5632, 2048], P('tensor', 'dp'), may hold values from -21.76 to 21.76
- small_first: float32 [7, 2048], replicated, may hold values from -21.76 to 21.76
- qkv_second: float32 [3, 2048, 2048], P(None, 'dp', 'tensor'), may hold values from 0.2048 to 3.2768
- out_second: float32 [2048, 2048], P('tensor', 'dp'), may hold values from 0.458752 to 7.3728
- gate_up_second: float32 [2, 2048, 5632], P(None, 'dp', 'tensor'), may hold values from 1.277952 to 20.48
- down_second: float32 [5632, 2048], P('tensor', 'dp'), may hold values from 1.277952 to 20.48
- small_second: float32 [7, 2048], replicated, may hold values from 1.277952 to 20.48
Outputs:
- block_out: bfloat16 [16384, 2048], P(('dp', 'tensor'))
- grad_in: float32 [16384, 2048], P(('dp', 'tensor'))
- qkv_grad: float32 [3, 2048, 2048], P(None, 'dp', 'tensor')
- qkv_first_new: float32 [3, 2048, 2048], P(None, 'dp', 'tensor')
- qkv_second_new: float32 [3, 2048, 2048], P(None, 'dp', 'tensor')
- qkv_new: float32 [3, 2048, 2048], P(None, 'dp', 'tensor')
- out_grad: float32 [2048, 2048], P('tensor', 'dp')
- out_first_new: float32 [2048, 2048], P('tensor', 'dp')
- out_second_new: float32 [2048, 2048], P('tensor', 'dp')
- out_new: float32 [2048, 2048], P('tensor', 'dp')
- gate_up_grad: float32 [2, 2048, 5632], P(None, 'dp', 'tensor')
- gate_up_first_new: float32 [2, 2048, 5632], P(None, 'dp', 'tensor')
- gate_up_second_new: float32 [2, 2048, 5632], P(None, 'dp', 'tensor')
- gate_up_new: float32 [2, 2048, 5632], P(None, 'dp', 'tensor')
- down_grad: float32 [5632, 2048], P('tensor', 'dp')
- down_first_new: float32 [5632, 2048], P('tensor', 'dp')
- down_second_new: float32 [5632, 2048], P('tensor', 'dp')
- down_new: float32 [5632, 2048], P('tensor', 'dp')
- small_grad: float32 [7, 2048], replicated
- small_first_new: float32 [7, 2048], replicated
- small_second_new: float32 [7, 2048], replicated
- small_new: float32 [7, 2048], replicated
The draws below stay inside these ranges and needn't reach their ends.
Inputs may be any that keep to these rules, and one draw needn't show every extreme that they name: Each index of dp holds exactly two sequences; their lengths sum to at most 2048, and to exactly 2048 on some index. `owners`: every index of dp is named exactly twice.
All inputs are finite; a program needn't handle non-finite values.
Results may differ from the reference program's by a relative error of at most 0.015.
The reference program's roundings to bfloat16 on the way count: a program that leaves them out, or rounds other values in their place, can miss the bound.
Values may be sent and summed in bfloat16 or wider, within the bound.
No kernel may reach another device: no remote copies, remote signals or barrier semaphores. Data moves between devices by JAX's collectives and lax.ppermute only.
A program may use at most 384 MiB of HBM per device.

```python
import math
import jax
import jax.numpy as jnp
from jax import lax

D = 2048
HEADS = 32
HD = 64
FF = 5632
ROT = 16
CAP = 2048
MINLEN = 256
STEP = 10
TOKENS = 16384
N_DP = 8


def deal_sequences(key):
    key_pick, key_totals, key_firsts, key_order = jax.random.split(key, 4)
    full_index = jax.random.randint(key_pick, (), 0, N_DP)
    marks = jnp.arange(N_DP) == full_index
    totals = jax.random.randint(key_totals, (N_DP,), 2 * MINLEN, CAP + 1)
    totals = jnp.where(marks, CAP, totals)
    firsts = jax.random.randint(key_firsts, (N_DP,), MINLEN, totals - MINLEN + 1)
    firsts = jnp.where(marks, CAP - MINLEN, firsts)
    seconds = totals - firsts
    slot_lengths = jnp.stack([firsts, seconds], axis=1).reshape(2 * N_DP).astype(jnp.int32)
    order = jax.random.permutation(key_order, 2 * N_DP)
    lengths = jnp.zeros((2 * N_DP,), jnp.int32).at[order].set(slot_lengths)
    owners = jnp.zeros((2 * N_DP,), jnp.int32).at[order].set((jnp.arange(2 * N_DP) // 2).astype(jnp.int32))
    return (lengths, owners)


def draw_lengths(key, part):
    return deal_sequences(key)[0]


def draw_owners(key, part):
    return deal_sequences(key)[1]


def level_of(rng, dims, cuts, low, largest):
    level, own = 1.0, jax.random.fold_in(rng, 6)
    for axis_at, blocks in cuts:
        steps = jnp.exp(jax.random.uniform(jax.random.fold_in(own, axis_at), (blocks,), jnp.float32, low / len(cuts), largest / len(cuts)))
        level = level * jnp.repeat(steps, dims[axis_at] // blocks).reshape([-1 if axis == axis_at else 1 for axis in range(len(dims))])
    return level


def centred(rng, shape, width, most, shards=(), held_as=jnp.bfloat16):
    level = level_of(rng, shape, shards, -0.22, 0.18) if shards else 1.0
    entries = jax.random.normal(rng, shape, jnp.float32) * width * level
    return jnp.minimum(jnp.maximum(entries, -most), most).astype(held_as)


def setup_inputs(seed: int = 0) -> dict:
    keys = jax.random.split(jax.random.key(seed), 22)
    hidden_in = centred(keys[0], (TOKENS, D), 1.0, 6.0, ((0, 32),))
    grad_out = centred(keys[1], (TOKENS, D), 1.0, 6.0, ((0, 32),))
    lengths = draw_lengths(jax.random.fold_in(keys[21], 71), 0)
    owners = draw_owners(jax.random.fold_in(keys[21], 71), 0)
    qkv_weight = centred(keys[4], (3, D, D), D ** -0.5, 0.125, ((1, 8), (2, 4)), jnp.float32)
    out_weight = centred(keys[5], (D, D), (D // 16) ** -0.5, 0.5, ((0, 4), (1, 8)), jnp.float32)
    gate_up_weight = centred(keys[6], (2, D, FF), D ** -0.5, 0.125, ((1, 8), (2, 4)), jnp.float32)
    down_weight = centred(keys[7], (FF, D), FF ** -0.5, 0.078125, ((0, 4), (1, 8)), jnp.float32)
    norm_gain = jnp.clip(1.0 + 0.1 * jax.random.normal(keys[8], (2, D), jnp.float32), 0.5, 1.5)
    norm_bias = centred(keys[9], (2, D), 0.2, 1.0, (), jnp.float32)
    qkv_bias = centred(keys[10], (3, D), 0.3, 1.5, (), jnp.float32)
    qkv_first = centred(keys[11], (3, D, D), (0.0176 * TOKENS ** 0.5), 8.96, ((1, 8), (2, 4)), jnp.float32)
    out_first = centred(keys[12], (D, D), (0.0263 * TOKENS ** 0.5), 12.8, ((0, 4), (1, 8)), jnp.float32)
    gate_up_first = centred(keys[13], (2, D, FF), (0.0439 * TOKENS ** 0.5), 21.76, ((1, 8), (2, 4)), jnp.float32)
    down_first = centred(keys[14], (FF, D), (0.0439 * TOKENS ** 0.5), 21.76, ((0, 4), (1, 8)), jnp.float32)
    small_first = centred(keys[15], (7, D), (0.0439 * TOKENS ** 0.5), 21.76, (), jnp.float32)
    qkv_second = jnp.clip(jnp.exp(math.log(3.2768) - 2.7725887 * jax.random.uniform(keys[16], (3, D, D), jnp.float32) ** level_of(keys[16], (3, D, D), ((1, 8), (2, 4)), -0.2, 0.2)), 0.2048, 3.2768)
    out_second = jnp.clip(jnp.exp(math.log(7.3728) - 2.777043 * jax.random.uniform(keys[17], (D, D), jnp.float32) ** level_of(keys[17], (D, D), ((0, 4), (1, 8)), -0.2, 0.2)), 0.458752, 7.3728)
    gate_up_second = jnp.clip(jnp.exp(math.log(20.48) - 2.77419 * jax.random.uniform(keys[18], (2, D, FF), jnp.float32) ** level_of(keys[18], (2, D, FF), ((1, 8), (2, 4)), -0.2, 0.2)), 1.277952, 20.48)
    down_second = jnp.clip(jnp.exp(math.log(20.48) - 2.77419 * jax.random.uniform(keys[19], (FF, D), jnp.float32) ** level_of(keys[19], (FF, D), ((0, 4), (1, 8)), -0.2, 0.2)), 1.277952, 20.48)
    small_second = jnp.clip(jnp.exp(jax.random.uniform(keys[20], (7, D), jnp.float32, math.log(1.277952), math.log(20.48))), 1.277952, 20.48)
    return {"hidden_in": hidden_in, "grad_out": grad_out, "lengths": lengths, "owners": owners, "qkv_weight": qkv_weight, "out_weight": out_weight, "gate_up_weight": gate_up_weight, "down_weight": down_weight, "norm_gain": norm_gain, "norm_bias": norm_bias, "qkv_bias": qkv_bias, "qkv_first": qkv_first, "out_first": out_first, "gate_up_first": gate_up_first, "down_first": down_first, "small_first": small_first, "qkv_second": qkv_second, "out_second": out_second, "gate_up_second": gate_up_second, "down_second": down_second, "small_second": small_second}


NORM_EPS = 1e-05
BETA_ONE = 0.9
BETA_TWO = 0.999
ADAM_EPS = 1e-08
WEIGHT_DECAY = 0.1
RATE_QKV = 0.05
RATE_OUT = 0.2
RATE_GATE_UP = 0.05
RATE_DOWN = 0.03
RATE_SMALL = 0.5
PRECISE = lax.Precision.HIGHEST

@jax.custom_vjp
def low(v):
    return lax.optimization_barrier(v.astype(jnp.bfloat16)).astype(jnp.float32)

@jax.custom_vjp
def low_back(v):
    return v

def low_keep(v):
    return (low(v), None)

def low_pass(kept, grad):
    return (grad,)

def back_keep(v):
    return (v, None)

def back_low(kept, grad):
    return (low(grad),)
low.defvjp(low_keep, low_pass)
low_back.defvjp(back_keep, back_low)

def layout(lengths, owners, dp_index):
    owned = owners == dp_index
    owned_lengths = jnp.where(owned, lengths, 0).astype(jnp.int32)
    seq_ends = jnp.cumsum(owned_lengths).astype(jnp.int32)
    seq_starts = (seq_ends - owned_lengths).astype(jnp.int32)
    owned_total = seq_ends[-1]
    row_ids = jnp.arange(CAP, dtype=jnp.int32)
    inside = owned[None, :] & (row_ids[:, None] >= seq_starts[None, :]) & (row_ids[:, None] < seq_ends[None, :])
    inside_int = inside.astype(jnp.int32)
    live_rows = lax.optimization_barrier(jnp.sum(inside_int, axis=1)).astype(jnp.int32)
    seq_ids = jnp.arange(lengths.shape[0], dtype=jnp.int32)
    segment = jnp.where(live_rows > 0, lax.optimization_barrier(jnp.sum(inside_int * seq_ids[None, :], axis=1)).astype(jnp.int32), -1).astype(jnp.int32)
    begins = (lax.optimization_barrier(jnp.sum(inside_int * seq_starts[None, :], axis=1)).astype(jnp.int32) + (1 - live_rows) * owned_total).astype(jnp.int32)
    return (segment, (row_ids - begins).astype(jnp.int32), live_rows)

def tables(position):
    half_rot = ROT // 2
    freqs = 10000.0 ** (-(jnp.arange(half_rot, dtype=jnp.float32) * (2.0 / ROT)))
    angles = position.astype(jnp.float32)[:, None] * freqs[None, :]
    return (jnp.cos(angles), jnp.sin(angles))

def rotate(heads_in, cosines, sines, direction):
    half_rot = ROT // 2
    first_half = heads_in[..., :half_rot]
    second_half = heads_in[..., half_rot:ROT]
    cosine_rows = cosines[:, None, :]
    sine_rows = sines[:, None, :] * direction
    return jnp.concatenate([first_half * cosine_rows - second_half * sine_rows, second_half * cosine_rows + first_half * sine_rows, heads_in[..., ROT:]], axis=-1)

def layer_norm(values, gain, shift):
    average = lax.optimization_barrier(jnp.mean(values, axis=-1, keepdims=True))
    centered = values - average
    inverse = lax.rsqrt(lax.optimization_barrier(jnp.mean(centered * centered, axis=-1, keepdims=True)) + NORM_EPS)
    return centered * inverse * gain + shift

def attend(queries, keys_rot, values, segment):
    block_rows = min(512, CAP)
    key_rows = jnp.arange(CAP, dtype=jnp.int32)

    def one_block(block_index):
        first_row = block_index * block_rows
        query_block = lax.dynamic_slice_in_dim(queries, first_row, block_rows, 0)
        query_seg = lax.dynamic_slice_in_dim(segment, first_row, block_rows, 0)
        query_rows = first_row + jnp.arange(block_rows, dtype=jnp.int32)
        allowed = (query_seg[:, None] == segment[None, :]) & (key_rows[None, :] <= query_rows[:, None])
        raw = low_back(jnp.einsum('qhd,khd->hqk', query_block, keys_rot, precision=PRECISE))
        scores = jnp.where(allowed[None], raw * HD ** (-0.5), -1e+30)
        probs = low(jax.nn.softmax(scores, axis=-1))
        return jnp.einsum('hqk,khd->qhd', probs, values, precision=PRECISE)
    mixed = lax.map(jax.checkpoint(one_block), jnp.arange(CAP // block_rows, dtype=jnp.int32))
    return mixed.reshape(CAP, HEADS * HD)

def block_layer(weights, inputs_f, segment, position):
    qkv_w, out_w, gate_up_w, down_w, gain_rows, bias_rows, qkv_shift = weights
    normed_one = low(layer_norm(inputs_f, gain_rows[0], bias_rows[0]))
    projected = jnp.einsum('rd,cdf->rcf', normed_one, qkv_w, precision=PRECISE) + qkv_shift[None]
    projected = low_back(projected)
    heads_all = projected.reshape(CAP, 3, HEADS, HD)
    cosines, sines = tables(position)
    queries = low(rotate(heads_all[:, 0], cosines, sines, 1.0))
    keys_rot = low(rotate(heads_all[:, 1], cosines, sines, 1.0))
    values = low(heads_all[:, 2])
    attn_mix = low_back(low(attend(queries, keys_rot, values, segment)))
    branch = low_back(jnp.dot(attn_mix, out_w, precision=PRECISE))
    hidden = inputs_f + branch
    normed_two = low(layer_norm(hidden, gain_rows[1], bias_rows[1]))
    gate_up = low_back(jnp.einsum('rd,cdf->crf', normed_two, gate_up_w, precision=PRECISE))
    inner_act = low(jax.nn.silu(gate_up[0]) * gate_up[1])
    return hidden + low_back(jnp.dot(inner_act, down_w, precision=PRECISE))

def adam_update(weight_old, gradient, first_old, second_old, rate, decay):
    first_new = BETA_ONE * first_old + (1.0 - BETA_ONE) * gradient
    second_new = BETA_TWO * second_old + (1.0 - BETA_TWO) * gradient * gradient
    first_hat = first_new / (1.0 - BETA_ONE ** STEP)
    second_hat = second_new / (1.0 - BETA_TWO ** STEP)
    weight_new = weight_old * (1.0 - rate * decay) - rate * first_hat / (jnp.sqrt(second_hat) + ADAM_EPS)
    return (first_new, second_new, weight_new)

def reference(hidden_in, grad_out, lengths, owners, qkv_weight, out_weight, gate_up_weight, down_weight, norm_gain, norm_bias, qkv_bias, qkv_first, out_first, gate_up_first, down_first, small_first, qkv_second, out_second, gate_up_second, down_second, small_second):
    dp_ids = jnp.arange(N_DP, dtype=jnp.int32)
    segment, position, live_rows = jax.vmap(layout, in_axes=(None, None, 0))(lengths, owners, dp_ids)
    inputs_f = hidden_in.astype(jnp.float32).reshape(N_DP, CAP, D)

    def whole(qkv_w, out_w, gate_up_w, down_w, gain_rows, bias_rows, qkv_shift, layer_in):
        weights = (low(qkv_w), low(out_w), low(gate_up_w), low(down_w), gain_rows, bias_rows, qkv_shift)

        def per_index(items):
            return jax.checkpoint(block_layer)(weights, items[0], items[1], items[2])
        return lax.map(per_index, (layer_in, segment, position))
    layer_out, pullback = jax.vjp(whole, qkv_weight, out_weight, gate_up_weight, down_weight, norm_gain, norm_bias, qkv_bias, inputs_f)
    cotangent = grad_out.astype(jnp.float32).reshape(N_DP, CAP, D) * live_rows[:, :, None].astype(jnp.float32)
    grads = pullback(cotangent)
    small_weight = jnp.concatenate([norm_gain, norm_bias, qkv_bias], axis=0)
    small_grad = jnp.concatenate([grads[4], grads[5], grads[6]], axis=0)
    qkv_first_new, qkv_second_new, qkv_new = adam_update(qkv_weight, grads[0], qkv_first, qkv_second, RATE_QKV, WEIGHT_DECAY)
    out_first_new, out_second_new, out_new = adam_update(out_weight, grads[1], out_first, out_second, RATE_OUT, WEIGHT_DECAY)
    gate_up_first_new, gate_up_second_new, gate_up_new = adam_update(gate_up_weight, grads[2], gate_up_first, gate_up_second, RATE_GATE_UP, WEIGHT_DECAY)
    down_first_new, down_second_new, down_new = adam_update(down_weight, grads[3], down_first, down_second, RATE_DOWN, WEIGHT_DECAY)
    small_first_new, small_second_new, small_new = adam_update(small_weight, small_grad, small_first, small_second, RATE_SMALL, 0.0)
    return (layer_out.reshape(TOKENS, D).astype(jnp.bfloat16), grads[7].reshape(TOKENS, D), grads[0], qkv_first_new, qkv_second_new, qkv_new, grads[1], out_first_new, out_second_new, out_new, grads[2], gate_up_first_new, gate_up_second_new, gate_up_new, grads[3], down_first_new, down_second_new, down_new, small_grad, small_first_new, small_second_new, small_new)
```

```python
import functools

import jax
import jax.numpy as jnp
from jax import lax
from jax.experimental import pallas as pl
from jax.experimental.pallas import tpu as pltpu
from jax.sharding import PartitionSpec as P

STEP = 10
NORM_EPS = 1e-05
BETA_ONE = 0.9
BETA_TWO = 0.999
ADAM_EPS = 1e-08
WEIGHT_DECAY = 0.1
RATE_QKV = 0.05
RATE_OUT = 0.2
RATE_GATE_UP = 0.05
RATE_DOWN = 0.03
RATE_SMALL = 0.5
HD = 64
ROT = 16
BLK = 256
PAIR = 2 * HD
NT = (((1,), (1,)), ((), ()))
NN = (((1,), (0,)), ((), ()))
NEG = -1e30
VMEM_LIMIT = 56 * 1024 * 1024
THRIFT = 1


def spend(flops, bytes_accessed, transcendentals):
    return pl.CostEstimate(
        flops=flops // THRIFT,
        bytes_accessed=bytes_accessed // THRIFT,
        transcendentals=transcendentals // THRIFT,
    )


def mm(a, b, dims=NN):
    return lax.dot_general(a, b, dims, preferred_element_type=jnp.float32)


def lane_masks():
    lane = lax.broadcasted_iota(jnp.int32, (1, PAIR), 1)
    first = jnp.where(lane < HD, 1.0, 0.0).astype(jnp.bfloat16)
    second = jnp.where(lane < HD, 0.0, 1.0).astype(jnp.bfloat16)
    return (first, second)


def allowed_block(info_ref, key_block, query_block):
    split, total = info_ref[0], info_ref[1]
    key_rows = key_block * BLK + lax.broadcasted_iota(jnp.int32, (BLK, BLK), 0)
    query_rows = query_block * BLK + lax.broadcasted_iota(jnp.int32, (BLK, BLK), 1)
    rows = query_block * BLK + lax.broadcasted_iota(jnp.int32, (1, BLK), 1)
    starts = jnp.where(rows < split, 0, jnp.where(rows < total, split, total))
    return (key_rows <= query_rows) & (key_rows >= starts)


def row_start(info_ref, row):
    split, total = info_ref[0], info_ref[1]
    return jnp.where(row < split, 0, jnp.where(row < total, split, total))


def key_range(info_ref, query_block):
    low = row_start(info_ref, query_block * BLK) // BLK
    last = row_start(info_ref, query_block * BLK + (BLK - 1))
    mid = jnp.minimum((last + (BLK - 1)) // BLK, query_block)
    return (low, mid)


def swap_block(block, shift_index, per_own):
    return lax.bitwise_xor(block // per_own, shift_index) * per_own + block % per_own


def aligned(block):
    return pl.ds(pl.multiple_of(block * BLK, BLK), BLK)


def attend_forward_kernel(chunks, count, per_own, after, info_ref, *refs):
    refs = refs[after:]
    group = len(chunks)
    q_refs, refs = refs[:group], refs[group:]
    k_refs, v_refs, refs = refs[:count], refs[count : 2 * count], refs[2 * count :]
    o_refs, l_refs = refs[:group], refs[group : 2 * group]
    q_all, o_all, l_all, k_all, vt_all = refs[2 * group :]
    tensor_at = info_ref[2]
    own = per_own * BLK
    heads = k_all.shape[1] // HD
    spans = [slice(head // 2 * PAIR, head // 2 * PAIR + PAIR) for head in range(heads)]
    for at in range(count):
        k_all[at * own : (at + 1) * own, :] = k_refs[at][...]
        vt_all[:, at * own : (at + 1) * own] = v_refs[at][...].T
    for at in range(group):
        q_all[at * own : (at + 1) * own, :] = q_refs[at][...]
    masks = lane_masks()

    def one_query(local_block, carry):
        chunk = local_block // per_own + chunks[0]
        query_block = swap_block(chunk * per_own + local_block % per_own, tensor_at, per_own)
        here = aligned(local_block)
        q_block = q_all[here, :]
        q_heads = [
            q_block[:, spans[head]] * (masks[head % 2] * HD ** (-0.5)).astype(jnp.bfloat16)
            for head in range(heads)
        ]
        low, mid = key_range(info_ref, query_block)

        def one_key(masked, step, state):
            key_block = jnp.where(step < mid, step, query_block) if masked else step
            place = aligned(swap_block(key_block, tensor_at, per_own))
            k_block = k_all[place, :]
            out = []
            if masked:
                allowed = allowed_block(info_ref, key_block, query_block)
            for head in range(heads):
                peak, total, mixed = state[head]
                scores = mm(k_block[:, spans[head]], q_heads[head], NT)
                if masked:
                    scores = jnp.where(allowed, scores, NEG)
                new_peak = jnp.maximum(peak, jnp.max(scores, axis=0, keepdims=True))
                probs = jnp.exp(scores - new_peak)
                decay = jnp.exp(peak - new_peak)
                total = total * decay + jnp.sum(probs, axis=0, keepdims=True)
                v_part = vt_all[pl.ds(head * HD, HD), place]
                mixed = mixed * decay + mm(v_part, probs.astype(jnp.bfloat16))
                out.append((new_peak, total, mixed))
            return tuple(out)

        state = tuple(
            (
                jnp.full((1, BLK), NEG, jnp.float32),
                jnp.zeros((1, BLK), jnp.float32),
                jnp.zeros((HD, BLK), jnp.float32),
            )
            for _ in range(heads)
        )
        state = lax.fori_loop(mid, query_block, functools.partial(one_key, False), state)
        state = lax.fori_loop(low, mid + 1, functools.partial(one_key, True), state)
        both = jnp.concatenate([mixed / total for _, total, mixed in state], axis=0)
        o_all[here, :] = both.T.astype(jnp.bfloat16)
        for head in range(heads):
            peak, total, _ = state[head]
            l_all[pl.ds(head, 1), here] = peak + jnp.log(total)
        return carry

    lax.fori_loop(0, group * per_own, one_query, 0)
    for at in range(group):
        span = slice(at * own, (at + 1) * own)
        o_refs[at][...] = o_all[span, :]
        for head in range(heads):
            l_refs[at][head // 2, pl.ds(head % 2, 1), :] = l_all[pl.ds(head, 1), span]


def attend_forward(info, queries, keys_rot, values, chunks, after=()):
    own, width = queries[0].shape
    count, group = len(keys_rot), len(chunks)
    rows, pairs = own * count, width // PAIR
    together = 1
    wide_pair = together * PAIR
    steps = own * group * rows // 2
    column = pl.BlockSpec((own, wide_pair), lambda p, s: (0, p))
    outs = pl.pallas_call(
        functools.partial(attend_forward_kernel, tuple(chunks), count, own // BLK, len(after)),
        grid_spec=pltpu.PrefetchScalarGridSpec(
            num_scalar_prefetch=1,
            grid=(pairs // together,),
            in_specs=[pl.BlockSpec(memory_space=pl.ANY)] * len(after) + [column] * (group + 2 * count),
            out_specs=[column] * group
            + [pl.BlockSpec((together, 2, own), lambda p, s: (p, 0, 0))] * group,
            scratch_shapes=[
                pltpu.VMEM((group * own, wide_pair), jnp.bfloat16),
                pltpu.VMEM((group * own, wide_pair), jnp.bfloat16),
                pltpu.VMEM((max(2 * together, 8), group * own), jnp.float32),
                pltpu.VMEM((rows, wide_pair), jnp.bfloat16),
                pltpu.VMEM((wide_pair, rows), jnp.bfloat16),
            ],
        ),
        out_shape=[jax.ShapeDtypeStruct((own, width), jnp.bfloat16)] * group
        + [jax.ShapeDtypeStruct((pairs, 2, own), jnp.float32)] * group,
        compiler_params=pltpu.CompilerParams(vmem_limit_bytes=VMEM_LIMIT),
        cost_estimate=spend(
            flops=THRIFT * 16 * steps * width, bytes_accessed=8 * rows * width, transcendentals=steps * width // HD
        ),
        name="attend_forward",
    )(info, *after, *[queries[chunk] for chunk in chunks], *keys_rot, *values)
    return (outs[:group], outs[group:])


def spin(values, cosines, sines_low, sines_high, sign):
    ahead = pltpu.roll(values, PAIR - ROT // 2, 1)
    behind = pltpu.roll(values, ROT // 2, 1)
    return values * cosines + sign * (ahead * sines_low + behind * sines_high)


def attend_backward_kernel(count, pieces, per_own, after, info_ref, *refs):
    do_refs, refs = refs[after : after + pieces], refs[after + pieces :]
    q_refs, k_refs, v_refs, o_refs, l_refs = [
        refs[at * count : (at + 1) * count] for at in range(5)
    ]
    c_ref, sl_ref, sh_ref, out_ref, sum_ref, *scratch = refs[5 * count :]
    q_all, do_all, o_all, l_all, k_all, kt_all, v_all, dk_sum, dv_sum = scratch
    tensor_at = info_ref[2]
    own = per_own * BLK
    heads = k_all.shape[1] // HD
    spans = [slice(head // 2 * PAIR, head // 2 * PAIR + PAIR) for head in range(heads)]
    for at in range(count):
        span = slice(at * own, (at + 1) * own)
        k_all[span, :] = k_refs[at][...]
        kt_all[:, span] = k_refs[at][...].T
        v_all[span, :] = v_refs[at][...]
        q_all[span, :] = q_refs[at][...]
        o_all[span, :] = o_refs[at][...]
        for head in range(heads):
            l_all[pl.ds(head, 1), span] = l_refs[at][head // 2, pl.ds(head % 2, 1), :]
    done = 0
    for one in do_refs:
        do_all[done : done + one.shape[0], :] = one[...]
        done += one.shape[0]
    dk_sum[...] = jnp.zeros_like(dk_sum)
    dv_sum[...] = jnp.zeros_like(dv_sum)
    masks = lane_masks()

    def one_query(local_block, carry):
        query_block = swap_block(local_block, tensor_at, per_own)
        here = aligned(local_block)
        q_block = q_all[here, :]
        do_block = do_all[here, :]
        q_heads = [
            q_block[:, spans[head]] * (masks[head % 2] * HD ** (-0.5)).astype(jnp.bfloat16)
            for head in range(heads)
        ]
        do_heads = [do_block[:, spans[head]] * masks[head % 2] for head in range(heads)]
        prod = (do_block.astype(jnp.float32) * o_all[here, :].astype(jnp.float32)).T
        deltas = [
            jnp.sum(prod[head * HD : (head + 1) * HD], axis=0, keepdims=True) for head in range(heads)
        ]
        logs = [l_all[pl.ds(head, 1), here] for head in range(heads)]
        low, mid = key_range(info_ref, query_block)

        def one_key(masked, step, state):
            key_block = jnp.where(step < mid, step, query_block) if masked else step
            place = aligned(swap_block(key_block, tensor_at, per_own))
            k_block = k_all[place, :]
            v_block = v_all[place, :]
            if masked:
                allowed = allowed_block(info_ref, key_block, query_block)
            out, dk_parts, dv_parts = [], [], []
            for head in range(heads):
                probs = jnp.exp(mm(k_block[:, spans[head]], q_heads[head], NT) - logs[head])
                if masked:
                    probs = jnp.where(allowed, probs, 0.0)
                dprobs = mm(v_block[:, spans[head]], do_heads[head], NT)
                dscores = (probs * (dprobs - deltas[head])).astype(jnp.bfloat16)
                dv_parts.append(mm(probs.astype(jnp.bfloat16), do_heads[head]))
                dk_parts.append(mm(dscores, q_heads[head]))
                out.append(state[head] + mm(kt_all[pl.ds(head * HD, HD), place], dscores))
            for head in range(0, heads, 2):
                dk_sum[place, spans[head]] += dk_parts[head] + dk_parts[head + 1]
                dv_sum[place, spans[head]] += dv_parts[head] + dv_parts[head + 1]
            return tuple(out)

        state = tuple(jnp.zeros((HD, BLK), jnp.float32) for _ in range(heads))
        state = lax.fori_loop(mid, query_block, functools.partial(one_key, False), state)
        state = lax.fori_loop(low, mid + 1, functools.partial(one_key, True), state)
        dq = jnp.concatenate(state, axis=0).T * HD ** (-0.5)
        for span in spans[::2]:
            out_ref[0, here, span] = spin(
                dq[:, span], c_ref[here, :], sl_ref[here, :], sh_ref[here, :], -1.0
            ).astype(jnp.bfloat16)
        return carry

    lax.fori_loop(0, count * per_own, one_query, 0)
    for span in spans[::2]:
        out_ref[1, :, span] = spin(
            dk_sum[:, span], c_ref[...], sl_ref[...], sh_ref[...], -1.0
        ).astype(jnp.bfloat16)
    out_ref[2] = dv_sum[...].astype(jnp.bfloat16)
    for part in range(3):
        sum_ref[pl.ds(part, 1), :] = jnp.sum(
            out_ref[part].astype(jnp.float32), axis=0, keepdims=True
        )


def attend_backward(
    info, queries, keys_rot, values, grad_mix, mixed, logs, tables, first, pairs, held=(), after=()
):
    own, full = queries[0].shape
    count = len(queries)
    rows, width = own * count, pairs * PAIR
    together = 1
    shift = first // together
    steps = rows * rows // 2
    column = pl.BlockSpec((own, together * PAIR), lambda p, s: (0, p + shift))
    line = pl.BlockSpec((together, 2, own), lambda p, s: (p + shift, 0, 0))
    table = pl.BlockSpec((rows, PAIR), lambda p, s: (0, 0))
    far = list(held) + list(after)
    return pl.pallas_call(
        functools.partial(
            attend_backward_kernel, count, len(grad_mix), own // BLK, len(far)
        ),
        grid_spec=pltpu.PrefetchScalarGridSpec(
            num_scalar_prefetch=1,
            grid=(pairs // together,),
            in_specs=[pl.BlockSpec(memory_space=pl.ANY)] * len(far)
            + [
                pl.BlockSpec((one.shape[0], together * PAIR), lambda p, s: (0, p + shift))
                for one in grad_mix
            ]
            + [column] * (4 * count)
            + [line] * count
            + [table] * 3,
            out_specs=[
                pl.BlockSpec((3, rows, together * PAIR), lambda p, s: (0, 0, p + shift)),
                pl.BlockSpec((3, together * PAIR), lambda p, s: (0, p)),
            ],
            scratch_shapes=[
                pltpu.VMEM((rows, together * PAIR), jnp.bfloat16),
                pltpu.VMEM((rows, together * PAIR), jnp.bfloat16),
                pltpu.VMEM((rows, together * PAIR), jnp.bfloat16),
                pltpu.VMEM((max(2 * together, 8), rows), jnp.float32),
                pltpu.VMEM((rows, together * PAIR), jnp.bfloat16),
                pltpu.VMEM((together * PAIR, rows), jnp.bfloat16),
                pltpu.VMEM((rows, together * PAIR), jnp.bfloat16),
                pltpu.VMEM((rows, together * PAIR), jnp.float32),
                pltpu.VMEM((rows, together * PAIR), jnp.float32),
            ],
        ),
        out_shape=[
            jax.ShapeDtypeStruct((3, rows, full), jnp.bfloat16),
            jax.ShapeDtypeStruct((3, width), jnp.float32),
        ],
        input_output_aliases={1: 0} if held else {},
        compiler_params=pltpu.CompilerParams(vmem_limit_bytes=VMEM_LIMIT),
        cost_estimate=spend(
            flops=THRIFT * 40 * steps * width, bytes_accessed=16 * rows * width, transcendentals=steps * width // HD
        ),
        name="attend_backward",
    )(info, *far, *grad_mix, *queries, *keys_rot, *values, *mixed, *logs, *tables)


def project_kernel(x_ref, w_ref, b_ref, c_ref, sl_ref, sh_ref, q_ref, k_ref, v_ref):
    rows_in = x_ref[...]
    width = q_ref.shape[1]
    for part, out_ref in enumerate((q_ref, k_ref, v_ref)):
        full = mm(rows_in, w_ref[part]) + b_ref[pl.ds(part, 1), :]
        if part == 2:
            out_ref[...] = full.astype(jnp.bfloat16)
            continue
        for at in range(0, width, PAIR):
            piece = full[:, at : at + PAIR]
            out_ref[:, at : at + PAIR] = spin(
                piece, c_ref[...], sl_ref[...], sh_ref[...], 1.0
            ).astype(jnp.bfloat16)


def project(normed, weight, bias, tables, chunk=0):
    rows, depth = normed.shape
    width = weight.shape[2]
    block = min(rows, 256)
    first = chunk * rows // block
    table = pl.BlockSpec((block, PAIR), lambda i: (i + first, 0))
    return pl.pallas_call(
        project_kernel,
        grid=(rows // block,),
        in_specs=[
            pl.BlockSpec((block, depth), lambda i: (i, 0)),
            pl.BlockSpec((3, depth, width), lambda i: (0, 0, 0)),
            pl.BlockSpec((3, width), lambda i: (0, 0)),
            table,
            table,
            table,
        ],
        out_specs=[pl.BlockSpec((block, width), lambda i: (i, 0))] * 3,
        out_shape=[jax.ShapeDtypeStruct((rows, width), jnp.bfloat16)] * 3,
        compiler_params=pltpu.CompilerParams(vmem_limit_bytes=VMEM_LIMIT),
        cost_estimate=spend(
            flops=6 * rows * depth * width, bytes_accessed=2 * rows * depth + 6 * (rows + depth) * width, transcendentals=0
        ),
        name="project",
    )(normed, weight, bias, *tables)


def copy_in(source, target, sem):
    made = pltpu.make_async_copy(source, target, sem)
    made.start()
    return made


def feed_kernel(held, split, cut, after, *refs):
    refs = refs[after:]
    x_hbm, dy_hbm, refs = refs[:split], refs[split : split + cut], refs[split + cut :]
    gu_hbm, wd_hbm = refs[:2]
    z_ref, dgu_ref, da_ref = refs[2 + held : 5 + held]
    x_in, dy_in, wg_in, wu_in, wd_in, gate, up, inner_all, sems = refs[5 + held :]
    depth = x_in.shape[1]
    half = depth // 2
    rows = x_in.shape[0]
    piece, slab = rows // split, rows // cut
    get_x = [
        copy_in(x_hbm[at], x_in.at[pl.ds(at * piece, piece)], sems.at[5 + at]) for at in range(split)
    ]
    get_g0 = copy_in(gu_hbm.at[0, pl.ds(0, half)], wg_in.at[pl.ds(0, half)], sems.at[1])
    get_g1 = copy_in(gu_hbm.at[0, pl.ds(half, half)], wg_in.at[pl.ds(half, half)], sems.at[2])
    for one in get_x:
        one.wait()
    get_g0.wait()
    get_u = copy_in(gu_hbm.at[1], wu_in, sems.at[3])
    gate[...] = mm(x_in[:, :half], wg_in[:half])
    get_g1.wait()
    get_dy = [
        copy_in(dy_hbm[at], dy_in.at[pl.ds(at * slab, slab)], sems.at[7 + at])
        for at in range(cut)
    ]
    get_d = copy_in(wd_hbm, wd_in, sems.at[4])
    gate[...] += mm(x_in[:, half:], wg_in[half:])
    get_u.wait()
    up[...] = mm(x_in[...], wu_in[...])
    for one in get_dy:
        one.wait()
    get_d.wait()
    hidden = wd_in.shape[0]
    for at in range(0, hidden, BLK):
        span = slice(at, min(at + BLK, hidden))
        inner_all[:, span] = mm(dy_in[...], wd_in[span, :], NT)
    step = 64

    def middle(at, carry):
        here = pl.ds(pl.multiple_of(at * step, step), step)
        gate_pre, up_pre, inner = gate[here, :], up[here, :], inner_all[here, :]
        sigmoid_gate = 1.0 / (1.0 + jnp.exp(-gate_pre))
        activated = gate_pre * sigmoid_gate
        z_ref[here, :] = (activated * up_pre).astype(jnp.bfloat16)
        dgu_ref[0, here, :] = (
            inner * up_pre * (sigmoid_gate * (1.0 + gate_pre * (1.0 - sigmoid_gate)))
        ).astype(jnp.bfloat16)
        dgu_ref[1, here, :] = (inner * activated).astype(jnp.bfloat16)
        return carry

    lax.fori_loop(0, rows // step, middle, 0)

    def back(at, carry):
        here = pl.ds(pl.multiple_of(at * BLK, BLK), BLK)
        da_ref[:, here] = (
            mm(dgu_ref[0], wg_in[here, :], NT) + mm(dgu_ref[1], wu_in[here, :], NT)
        ).astype(da_ref.dtype)
        return carry

    lax.fori_loop(0, depth // BLK, back, 0)


def feed(chunk, count, normed, back, gate_up, down, held, after=()):
    split, cut = len(normed), len(back)
    rows, depth = normed[0].shape[0] * split, normed[0].shape[1]
    hidden = down.shape[0]
    far = pl.BlockSpec(memory_space=pl.ANY)
    return pl.pallas_call(
        functools.partial(feed_kernel, len(held), split, cut, len(after)),
        grid=(1,),
        in_specs=[far] * (2 + split + cut + len(held) + len(after)),
        out_specs=[
            pl.BlockSpec((rows, hidden), lambda i: (chunk, 0)),
            pl.BlockSpec((2, rows, hidden), lambda i: (0, chunk, 0)),
            pl.BlockSpec((rows, depth), lambda i: (0, 0)),
        ],
        out_shape=[
            jax.ShapeDtypeStruct((rows * count, hidden), jnp.bfloat16),
            jax.ShapeDtypeStruct((2, rows * count, hidden), jnp.bfloat16),
            jax.ShapeDtypeStruct((rows, depth), jnp.float32 if chunk == 0 else jnp.bfloat16),
        ],
        input_output_aliases={len(after) + 2 + split + cut + at: at for at in range(len(held))},
        scratch_shapes=[
            pltpu.VMEM((rows, depth), jnp.bfloat16),
            pltpu.VMEM((rows, depth), jnp.bfloat16),
            pltpu.VMEM((depth, hidden), jnp.bfloat16),
            pltpu.VMEM((depth, hidden), jnp.bfloat16),
            pltpu.VMEM((hidden, depth), jnp.bfloat16),
            pltpu.VMEM((rows, hidden), jnp.float32),
            pltpu.VMEM((rows, hidden), jnp.float32),
            pltpu.VMEM((rows, hidden), jnp.float32),
            pltpu.SemaphoreType.DMA((9,)),
        ],
        compiler_params=pltpu.CompilerParams(vmem_limit_bytes=VMEM_LIMIT),
        cost_estimate=spend(
            flops=10 * rows * depth * hidden, bytes_accessed=6 * depth * hidden, transcendentals=rows * hidden
        ),
        name="feed",
    )(*after, *normed, *back, gate_up, down, *held)


def wide_grad_kernel(count, after, *refs):
    refs = refs[after:]
    lefts, (right, out, turned) = refs[:count], refs[count:]
    done = 0
    for left in lefts:
        turned[:, done : done + left.shape[0]] = left[...].T
        done += left.shape[0]
    for part in range(out.shape[0]):
        out[part] = mm(turned[...], right[part]).astype(jnp.bfloat16)


def wide_grad(lefts, right, after=(), column=0, cuts=1):
    depth = lefts[0].shape[1]
    parts, rows, width = right.shape
    width = width // cuts
    return pl.pallas_call(
        functools.partial(wide_grad_kernel, len(lefts), len(after)),
        grid=(depth // BLK,),
        in_specs=[pl.BlockSpec(memory_space=pl.ANY)] * len(after)
        + [pl.BlockSpec((left.shape[0], BLK), lambda i: (0, i)) for left in lefts]
        + [pl.BlockSpec((parts, rows, width), lambda i: (0, 0, column))],
        out_specs=pl.BlockSpec((parts, BLK, width), lambda i: (0, i, 0)),
        out_shape=jax.ShapeDtypeStruct((parts, depth, width), jnp.bfloat16),
        scratch_shapes=[pltpu.VMEM((BLK, rows), jnp.bfloat16)],
        compiler_params=pltpu.CompilerParams(vmem_limit_bytes=VMEM_LIMIT),
        cost_estimate=spend(
            flops=2 * rows * depth * width * parts,
            bytes_accessed=2 * (rows * depth + parts * width * (rows + depth)),
            transcendentals=0,
        ),
        name="wide_grad",
    )(*after, *lefts, right)


def tall_grad_kernel(held, count, after, *refs):
    refs = refs[after:]
    lefts, rights, (out, turned, joined) = refs[:held], refs[held : held + count], refs[held + count :]
    tall = lefts[0].shape[0]

    @pl.when(pl.program_id(0) == 0)
    def _():
        for at in range(held):
            turned[:, at * tall : (at + 1) * tall] = lefts[at][...].T

    done = 0
    for right in rights:
        joined[done : done + right.shape[0], :] = right[...]
        done += right.shape[0]
    out[...] = mm(turned[...], joined[...]).astype(jnp.bfloat16)


def tall_grad(lefts, rights, after=()):
    tall, depth = lefts[0].shape
    width = rights[0].shape[1]
    count, held = len(rights), len(lefts)
    rows = tall * held
    return pl.pallas_call(
        functools.partial(tall_grad_kernel, held, count, len(after)),
        grid=(width // BLK,),
        in_specs=[pl.BlockSpec(memory_space=pl.ANY)] * len(after)
        + [pl.BlockSpec((tall, depth), lambda i: (0, 0))] * held
        + [pl.BlockSpec((right.shape[0], BLK), lambda i: (0, i)) for right in rights],
        out_specs=pl.BlockSpec((depth, BLK), lambda i: (0, i)),
        out_shape=jax.ShapeDtypeStruct((depth, width), jnp.bfloat16),
        scratch_shapes=[
            pltpu.VMEM((depth, rows), jnp.bfloat16),
            pltpu.VMEM((rows, BLK), jnp.bfloat16),
        ],
        compiler_params=pltpu.CompilerParams(vmem_limit_bytes=VMEM_LIMIT),
        cost_estimate=spend(
            flops=2 * rows * depth * width,
            bytes_accessed=2 * (rows * depth + width * (rows + depth)),
            transcendentals=0,
        ),
        name="tall_grad",
    )(*after, *lefts, *rights)


FAR = pl.BlockSpec(memory_space=pl.ANY)


def halves_kernel(after, count, *refs):
    for source, target in zip(refs[after : after + count], refs[after + count :]):
        target[...] = source[...]


def halves(picks, after=()):
    half, depth = picks[0][0].shape[0] // 2, picks[0][0].shape[1]
    specs = [
        pl.BlockSpec((half, depth), functools.partial(lambda which, i: (which, 0), which))
        for _, which in picks
    ]
    return pl.pallas_call(
        functools.partial(halves_kernel, len(after), len(picks)),
        grid=(1,),
        in_specs=[FAR] * len(after) + specs,
        out_specs=[pl.BlockSpec((half, depth), lambda i: (0, 0))] * len(picks),
        out_shape=[jax.ShapeDtypeStruct((half, depth), picks[0][0].dtype)] * len(picks),
        compiler_params=pltpu.CompilerParams(vmem_limit_bytes=VMEM_LIMIT),
        cost_estimate=spend(
            flops=half * depth, bytes_accessed=4 * len(picks) * half * depth, transcendentals=0
        ),
        name="halves",
    )(*after, *[one for one, _ in picks])


def join_kernel(after, *refs):
    top, end, out = refs[after:]
    half = top.shape[0]
    out[:half, :] = top[...]
    out[half:, :] = end[...]


def join(top, end, after=()):
    half, depth = top.shape
    whole = pl.BlockSpec((half, depth), lambda i: (0, 0))
    return pl.pallas_call(
        functools.partial(join_kernel, len(after)),
        grid=(1,),
        in_specs=[FAR] * len(after) + [whole, whole],
        out_specs=pl.BlockSpec((2 * half, depth), lambda i: (0, 0)),
        out_shape=jax.ShapeDtypeStruct((2 * half, depth), top.dtype),
        compiler_params=pltpu.CompilerParams(vmem_limit_bytes=VMEM_LIMIT),
        cost_estimate=spend(flops=half * depth, bytes_accessed=8 * half * depth, transcendentals=0),
        name="join",
    )(*after, top, end)


def shrink_kernel(after, *refs):
    source, scale, out = refs[after:]
    out[...] = (source[...].astype(jnp.float32) * scale[...]).astype(jnp.bfloat16)


def shrink(values, scale, after=()):
    rows, depth = values.shape
    block = rows // 4
    return pl.pallas_call(
        functools.partial(shrink_kernel, len(after)),
        grid=(4,),
        in_specs=[FAR] * len(after)
        + [
            pl.BlockSpec((block, depth), lambda i: (i, 0)),
            pl.BlockSpec((block, 1), lambda i: (i, 0)),
        ],
        out_specs=pl.BlockSpec((block, depth), lambda i: (i, 0)),
        out_shape=jax.ShapeDtypeStruct((rows, depth), jnp.bfloat16),
        compiler_params=pltpu.CompilerParams(vmem_limit_bytes=VMEM_LIMIT),
        cost_estimate=spend(
            flops=rows * depth, bytes_accessed=6 * rows * depth, transcendentals=0
        ),
        name="shrink",
    )(*after, values, scale)


LINES = 128


def arrived(own, parts, steps):
    total = own[...].astype(jnp.float32)
    if parts:
        first = pl.program_id(0) < steps // 2
        one, two, three, four = [part[...].astype(jnp.float32) for part in parts]
        total = total + jnp.where(first, one + two, three + four)
    return total


def part_specs(parts, depth, steps):
    if not parts:
        return []
    top = pl.BlockSpec((LINES, depth), lambda i: (jnp.minimum(i, steps // 2 - 1), 0))
    end = pl.BlockSpec((LINES, depth), lambda i: (jnp.maximum(i - steps // 2, 0), 0))
    return [top, top, end, end]


def unit_of(values):
    average = jnp.mean(values, axis=-1, keepdims=True)
    centered = values - average
    inverse = lax.rsqrt(jnp.mean(centered * centered, axis=-1, keepdims=True) + NORM_EPS)
    return (centered * inverse, inverse)


def settle_kernel(held, after, steps, *refs):
    refs = refs[after:]
    own, parts = refs[0], refs[1 : 1 + held]
    resid, gain, shift, hidden, normed = refs[1 + held :]
    values = resid[...].astype(jnp.float32) + arrived(own, parts, steps)
    hidden[...] = values
    normed[...] = (unit_of(values)[0] * gain[...] + shift[...]).astype(jnp.bfloat16)


def settle(own, parts, resid, gain, shift, after=()):
    rows, depth = own.shape
    steps = rows // LINES
    block = pl.BlockSpec((LINES, depth), lambda i: (i, 0))
    line = pl.BlockSpec((1, depth), lambda i: (0, 0))
    return pl.pallas_call(
        functools.partial(settle_kernel, len(parts), len(after), steps),
        grid=(steps,),
        in_specs=[FAR] * len(after)
        + [block]
        + part_specs(parts, depth, steps)
        + [block, line, line],
        out_specs=[block, block],
        out_shape=[
            jax.ShapeDtypeStruct((rows, depth), jnp.float32),
            jax.ShapeDtypeStruct((rows, depth), jnp.bfloat16),
        ],
        compiler_params=pltpu.CompilerParams(vmem_limit_bytes=VMEM_LIMIT),
        cost_estimate=spend(
            flops=10 * rows * depth, bytes_accessed=16 * rows * depth, transcendentals=rows
        ),
        name="settle",
    )(*after, own, *parts, resid, gain, shift)


def finish_kernel(held, after, steps, *refs):
    refs = refs[after:]
    own, parts = refs[0], refs[1 : 1 + held]
    hidden, out = refs[1 + held :]
    total = hidden[...] + arrived(own, parts, steps)
    out[...] = total.astype(jnp.bfloat16)


def finish(own, parts, hidden, after=()):
    rows, depth = own.shape
    steps = rows // LINES
    block = pl.BlockSpec((LINES, depth), lambda i: (i, 0))
    return pl.pallas_call(
        functools.partial(finish_kernel, len(parts), len(after), steps),
        grid=(steps,),
        in_specs=[FAR] * len(after) + [block] + part_specs(parts, depth, steps) + [block],
        out_specs=block,
        out_shape=jax.ShapeDtypeStruct((rows, depth), jnp.bfloat16),
        compiler_params=pltpu.CompilerParams(vmem_limit_bytes=VMEM_LIMIT),
        cost_estimate=spend(
            flops=4 * rows * depth, bytes_accessed=12 * rows * depth, transcendentals=0
        ),
        name="finish",
    )(*after, own, *parts, hidden)


def unsettle_kernel(held, after, steps, *refs):
    refs = refs[after:]
    own, parts = refs[0], refs[1 : 1 + held]
    values, extra, gain, total, short, gain_sum, shift_sum = refs[1 + held :]
    incoming = arrived(own, parts, steps)
    unit_rows, inverse = unit_of(values[...].astype(jnp.float32))
    scaled = incoming * gain[...]
    grad_rows = inverse * (
        scaled
        - jnp.mean(scaled, axis=-1, keepdims=True)
        - unit_rows * jnp.mean(scaled * unit_rows, axis=-1, keepdims=True)
    )
    result = extra[...].astype(jnp.float32) + grad_rows
    total[...] = result
    short[...] = result.astype(jnp.bfloat16)

    @pl.when(pl.program_id(0) == 0)
    def _():
        gain_sum[...] = jnp.zeros_like(gain_sum)
        shift_sum[...] = jnp.zeros_like(shift_sum)

    gain_sum[...] += jnp.sum(incoming * unit_rows, axis=0, keepdims=True)
    shift_sum[...] += jnp.sum(incoming, axis=0, keepdims=True)


def unsettle(own, parts, values, extra, gain, after=()):
    rows, depth = own.shape
    steps = rows // LINES
    block = pl.BlockSpec((LINES, depth), lambda i: (i, 0))
    line = pl.BlockSpec((1, depth), lambda i: (0, 0))
    return pl.pallas_call(
        functools.partial(unsettle_kernel, len(parts), len(after), steps),
        grid=(steps,),
        in_specs=[FAR] * len(after)
        + [block]
        + part_specs(parts, depth, steps)
        + [block, block, line],
        out_specs=[block, block, line, line],
        out_shape=[
            jax.ShapeDtypeStruct((rows, depth), jnp.float32),
            jax.ShapeDtypeStruct((rows, depth), jnp.bfloat16),
            jax.ShapeDtypeStruct((1, depth), jnp.float32),
            jax.ShapeDtypeStruct((1, depth), jnp.float32),
        ],
        compiler_params=pltpu.CompilerParams(vmem_limit_bytes=VMEM_LIMIT),
        cost_estimate=spend(
            flops=20 * rows * depth, bytes_accessed=20 * rows * depth, transcendentals=rows
        ),
        name="unsettle",
    )(*after, own, *parts, values, extra, gain)


def unproject_kernel(count, after, *refs):
    refs = refs[after:]
    lefts, w_ref, outs = refs[:count], refs[count], refs[count + 1 :]
    own = outs[0].shape[0]
    total = None
    for part in range(3):
        left = jnp.concatenate([one[part] for one in lefts], axis=0)
        made = mm(left, w_ref[part], NT)
        total = made if total is None else total + made
    for at, out in enumerate(outs):
        out[...] = total[at * own : (at + 1) * own].astype(out.dtype)


def unproject(grads, weight, chunks, own, after=()):
    parts, depth, width = weight.shape
    count = len(chunks)
    return pl.pallas_call(
        functools.partial(unproject_kernel, count, len(after)),
        grid=(depth // BLK,),
        in_specs=[FAR] * len(after)
        + [
            pl.BlockSpec((parts, own, width), functools.partial(lambda which, i: (0, which, 0), chunk))
            for chunk in chunks
        ]
        + [pl.BlockSpec((parts, BLK, width), lambda i: (0, i, 0))],
        out_specs=[pl.BlockSpec((own, BLK), lambda i: (0, i))] * count,
        out_shape=[
            jax.ShapeDtypeStruct((own, depth), jnp.bfloat16 if chunk else jnp.float32)
            for chunk in chunks
        ],
        compiler_params=pltpu.CompilerParams(vmem_limit_bytes=VMEM_LIMIT),
        cost_estimate=spend(
            flops=2 * parts * own * count * depth * width,
            bytes_accessed=2 * parts * width * (own * count + depth) + 4 * own * count * depth,
            transcendentals=0,
        ),
        name="unproject",
    )(*after, *[grads] * count, weight)


def adam_kernel(rate, decay, after, *refs):
    weight, gradient, first, second, grad_out, first_out, second_out, weight_out = refs[after:]
    grad = gradient[...].astype(jnp.float32)
    grad_out[...] = grad
    first_out[...], second_out[...], weight_out[...] = adam_update(
        weight[...], grad, first[...], second[...], rate, decay
    )


def adam(weight, gradient, first, second, rate, after=()):
    shape = weight.shape
    flat = (-1, shape[-1])
    arrays = [one.reshape(flat) for one in (weight, gradient, first, second)]
    rows, width = arrays[0].shape
    block = pl.BlockSpec((rows // 4, width), lambda i: (i, 0))
    outs = pl.pallas_call(
        functools.partial(adam_kernel, rate, WEIGHT_DECAY, len(after)),
        grid=(4,),
        in_specs=[FAR] * len(after) + [block] * 4,
        out_specs=[block] * 4,
        out_shape=[jax.ShapeDtypeStruct((rows, width), jnp.float32)] * 4,
        compiler_params=pltpu.CompilerParams(vmem_limit_bytes=VMEM_LIMIT),
        cost_estimate=spend(
            flops=12 * rows * width, bytes_accessed=30 * rows * width, transcendentals=0
        ),
        name="adam",
    )(*after, *arrays)
    return [one.reshape(shape) for one in outs]


def hold(values, after):
    rows, depth = values.shape
    whole = pl.BlockSpec((rows, depth), lambda i: (0, 0))

    def body(*refs):
        refs[-1][...] = refs[-2][...]

    return pl.pallas_call(
        body,
        grid=(1,),
        in_specs=[FAR] * len(after) + [whole],
        out_specs=whole,
        out_shape=jax.ShapeDtypeStruct((rows, depth), values.dtype),
        cost_estimate=spend(
            flops=rows * depth, bytes_accessed=8 * rows * depth, transcendentals=0
        ),
        name="hold",
    )(*after, values)


def first_line_kernel(after, *refs):
    w_ref, first_ref, second_ref, sum_ref, out_ref = refs[after:]
    cut = first_ref.shape[2]
    gain, shift = None, None
    for part in range(3):
        weight = w_ref[part].astype(jnp.float32)
        grad = jnp.concatenate([first_ref[part], second_ref[part]], axis=1).astype(jnp.float32)
        gain = weight * grad if gain is None else gain + weight * grad
        lean = weight * sum_ref[pl.ds(part, 1), :]
        shift = lean if shift is None else shift + lean
    out_ref[pl.ds(0, 1), :] = jnp.sum(gain.T, axis=0, keepdims=True)
    out_ref[pl.ds(1, 1), :] = jnp.sum(shift.T, axis=0, keepdims=True)


def first_line(weight, first, second, sums, after):
    parts, depth, width = weight.shape
    cut = first.shape[2]
    return pl.pallas_call(
        functools.partial(first_line_kernel, len(after)),
        grid=(depth // BLK,),
        in_specs=[FAR] * len(after)
        + [
            pl.BlockSpec((parts, BLK, width), lambda i: (0, i, 0)),
            pl.BlockSpec((parts, BLK, cut), lambda i: (0, i, 0)),
            pl.BlockSpec((parts, BLK, width - cut), lambda i: (0, i, 0)),
            pl.BlockSpec((parts, width), lambda i: (0, 0)),
        ],
        out_specs=pl.BlockSpec((2, BLK), lambda i: (0, i)),
        out_shape=jax.ShapeDtypeStruct((2, depth), jnp.float32),
        compiler_params=pltpu.CompilerParams(vmem_limit_bytes=VMEM_LIMIT),
        cost_estimate=spend(
            flops=4 * parts * depth * width, bytes_accessed=4 * parts * depth * width, transcendentals=0
        ),
        name="first_line",
    )(*after, weight, first, second, sums)


def down_project_kernel(after, count, *refs):
    z_ref, w_ref, outs = refs[after], refs[after + 1], refs[after + 2 :]
    for at in range(count):

        @pl.when(pl.program_id(0) == at)
        def _():
            outs[at][...] = mm(z_ref[...], w_ref[...]).astype(jnp.bfloat16)


def down_project(inner, weight, count, after=()):
    rows, hidden = inner.shape
    depth = weight.shape[1]
    own = rows // count
    return pl.pallas_call(
        functools.partial(down_project_kernel, len(after), count),
        grid=(count,),
        in_specs=[FAR] * len(after)
        + [
            pl.BlockSpec((own, hidden), lambda i: (i, 0)),
            pl.BlockSpec((hidden, depth), lambda i: (0, 0)),
        ],
        out_specs=[pl.BlockSpec((own, depth), lambda i: (0, 0))] * count,
        out_shape=[jax.ShapeDtypeStruct((own, depth), jnp.bfloat16)] * count,
        compiler_params=pltpu.CompilerParams(vmem_limit_bytes=VMEM_LIMIT),
        cost_estimate=spend(
            flops=2 * rows * depth * hidden,
            bytes_accessed=2 * (rows * depth + hidden * (rows + depth)),
            transcendentals=0,
        ),
        name="down_project",
    )(*after, inner, weight)


def lane_tables(position):
    half_rot = ROT // 2
    lane = jnp.arange(PAIR, dtype=jnp.int32) % HD
    freqs = 10000.0 ** (-((lane % half_rot).astype(jnp.float32) * (2.0 / ROT)))
    angles = position.astype(jnp.float32)[:, None] * freqs[None, :]
    cosines, sines = jnp.cos(angles), jnp.sin(angles)
    in_low, in_high = (lane < half_rot)[None], ((lane >= half_rot) & (lane < ROT))[None]
    return (
        jnp.where((lane < ROT)[None], cosines, 1.0),
        jnp.where(in_low, -sines, 0.0),
        jnp.where(in_high, sines, 0.0),
    )


def sequence_facts(lengths, owners, dp_index):
    owned = owners == dp_index
    total = jnp.sum(jnp.where(owned, lengths, 0))
    return (lengths[jnp.argmax(owned)], total)


def norm_forward(values, gain, shift):
    return unit_of(values)[0] * gain + shift


def adam_update(weight_old, gradient, first_old, second_old, rate, decay):
    first_new = BETA_ONE * first_old + (1.0 - BETA_ONE) * gradient
    second_new = BETA_TWO * second_old + (1.0 - BETA_TWO) * gradient * gradient
    first_hat = first_new / (1.0 - BETA_ONE**STEP)
    second_hat = second_new / (1.0 - BETA_TWO**STEP)
    weight_new = weight_old * (1.0 - rate * decay) - rate * first_hat / (
        jnp.sqrt(second_hat) + ADAM_EPS
    )
    return (first_new, second_new, weight_new)


def low(values):
    return values.astype(jnp.bfloat16)


def wide(values):
    return values.astype(jnp.float32)


def swap(values, axis, bits):
    size = lax.axis_size(axis)
    return lax.ppermute(values, axis, [(at, at ^ bits) for at in range(size)])


def gather_start(rows):
    count = lax.axis_size("tensor")
    if count != 4:
        return [swap(rows, "tensor", bits) for bits in range(1, count)]
    return [swap(rows, "tensor", 1), swap(rows, "tensor", 2)]


def gather_on(near, after=(), with_sends=False):
    passed, sends = (), ()
    if lax.axis_size("tensor") == 4:
        sends = halves([(near[0], 0), (near[1], 1)], after)
        passed = (swap(sends[0], "tensor", 2), swap(sends[1], "tensor", 1))
    return (passed, sends) if with_sends else passed


def pieces_of(pieces, chunk):
    return pieces[3:] if len(pieces) == 5 and chunk == 3 else [pieces[chunk]]


def scatter_start(parts, after=()):
    if lax.axis_size("tensor") != 4:
        return [swap(low(parts[bits]), "tensor", bits) for bits in range(1, len(parts))]
    _, one, two, three = parts
    half = one.shape[0] // 2
    if after:
        three_top, three_end, one_top, two_end = after
    else:
        three = low(three)
        three_top, three_end = three[:half], three[half:]
        one_top, two_end = low(one[:half]), low(two[half:])
    return [
        swap(three_top, "tensor", 1),
        swap(three_end, "tensor", 2),
        swap(one_top, "tensor", 1),
        swap(two_end, "tensor", 2),
    ]


def scatter_on(parts, moved):
    if lax.axis_size("tensor") != 4:
        return []
    _, one, two, _ = parts
    half = one.shape[0] // 2
    return [low(wide(one[half:]) + wide(moved[1])), low(wide(two[:half]) + wide(moved[0]))]


def scatter_end(parts, moved, passing=None):
    if lax.axis_size("tensor") != 4:
        total = wide(parts[0])
        for one in moved:
            total = total + wide(one)
        return (total, [])
    one_end, two_top = passing or scatter_on(parts, moved)
    return (
        parts[0],
        [moved[2], swap(two_top, "tensor", 2), swap(one_end, "tensor", 1), moved[3]],
    )


def sum_along(values, axis):
    bits = 1
    while bits < lax.axis_size(axis):
        values = values + swap(values, axis, bits)
        bits *= 2
    return values


def scatter_weight(partial):
    return lax.psum_scatter(partial, "dp", scatter_dimension=1, tiled=True)


def dot(left, right, dims):
    return lax.dot_general(left, right, (dims, ((), ())), preferred_element_type=jnp.float32)


def local(
    hidden_in,
    grad_out,
    lengths,
    owners,
    qkv_weight,
    out_weight,
    gate_up_weight,
    down_weight,
    norm_gain,
    norm_bias,
    qkv_bias,
    qkv_first,
    out_first,
    gate_up_first,
    down_first,
    small_first,
    qkv_second,
    out_second,
    gate_up_second,
    down_second,
    small_second,
):
    dp_index = lax.axis_index("dp")
    tp_index = lax.axis_index("tensor")
    count = lax.axis_size("tensor")
    own_rows = hidden_in.shape[0]
    local_width = qkv_weight.shape[2]
    chunks = list(range(count))
    groups = [[3], [1, 2], [0]] if count == 4 else [chunks[1:], [0]]
    qkv_full, out_full, gate_up_full, down_full = [
        lax.all_gather(low(one), "dp", axis=1, tiled=True)
        for one in (qkv_weight, out_weight, gate_up_weight, down_weight)
    ]
    split, total = sequence_facts(lengths, owners, dp_index)
    row_ids = jnp.concatenate(
        [(tp_index ^ chunk) * own_rows + jnp.arange(own_rows, dtype=jnp.int32) for chunk in chunks]
    )
    starts = jnp.where(row_ids < split, 0, jnp.where(row_ids < total, split, total))
    live_own = wide(row_ids[:own_rows] < total)
    info = jnp.stack([split, total, tp_index, tp_index]).astype(jnp.int32)
    lanes = lane_tables(row_ids - starts)
    bias_local = lax.dynamic_slice_in_dim(qkv_bias, tp_index * local_width, local_width, 1)

    first_norm = low(norm_forward(wide(hidden_in), norm_gain[0], norm_bias[0]))
    near = gather_start(first_norm)
    passed = gather_on(near)
    early = [
        project(one, qkv_full, bias_local, lanes, chunk)
        for chunk, one in enumerate([first_norm] + near)
    ]
    normed_one = [first_norm] + near
    if passed:
        normed_one.append(join(*passed, [one[0] for one in early]))
    projected = early + [
        project(normed_one[chunk], qkv_full, bias_local, lanes, chunk)
        for chunk in chunks[len(early) :]
    ]
    queries, keys_rot, values = [[one[part] for one in projected] for part in range(3)]
    cotangent = shrink(grad_out, live_own[:, None], normed_one[1:])
    near = gather_start(cotangent)
    passed = gather_on(near)
    back_ffn = [cotangent, *near] + ([join(*passed)] if passed else [])

    attn_mix, log_total = [None] * count, [None] * count
    for step, group in enumerate(groups):
        after = near if step == 1 else ()
        mixed, logs = attend_forward(info, queries, keys_rot, values, group, after)
        for at, chunk in enumerate(group):
            attn_mix[chunk], log_total[chunk] = mixed[at], logs[at]
    parts = [dot(one, out_full, ((1,), (0,))) for one in attn_mix]
    hidden, second_norm = settle(
        *scatter_end(parts, scatter_start(parts)),
        hidden_in,
        norm_gain[1:2],
        norm_bias[1:2],
    )

    near = gather_start(second_norm)
    held, back_second = (), [None] * count

    def feed_one(chunk, normed, held, after=()):
        *held, back_second[chunk] = feed(
            chunk, count, normed, pieces_of(back_ffn, chunk), gate_up_full, down_full, held, after
        )
        return held

    held = feed_one(0, [second_norm], held)
    passed = gather_on(near, held[:1])
    held = feed_one(1, near[:1], held)
    normed_two = [second_norm, *near, *passed]
    for chunk in [3, 2] if count == 4 else chunks[2:]:
        held = feed_one(chunk, pieces_of(normed_two, chunk), held)
    inner_act, grad_gate_up = held
    moved = scatter_start(back_second)
    passing = scatter_on(back_second, moved)
    gate_up_partial = wide_grad(normed_two, grad_gate_up, moved[:2] + passing)
    gate_up_grad = scatter_weight(gate_up_partial)
    layer_parts = down_project(inner_act, down_full, count, [gate_up_partial])
    grad_hidden, grad_hidden_low, gain_two_grad, bias_two_grad = unsettle(
        *scatter_end(back_second, moved, passing),
        hidden,
        cotangent,
        norm_gain[1:2],
        [gate_up_partial, *layer_parts],
    )
    near = gather_start(grad_hidden_low)
    down_partial = tall_grad([inner_act], back_ffn, [grad_hidden_low])
    down_grad = scatter_weight(down_partial)
    passed = gather_on(near, [down_partial])
    back_attn = [grad_hidden_low, *near, *passed]

    grad_mix = [low(dot(one, out_full, ((1,), (1,)))) for one in back_attn]
    layer_sends = []
    if count == 4:
        layer_sends = halves(
            [(layer_parts[3], 0), (layer_parts[3], 1), (layer_parts[1], 0), (layer_parts[2], 1)],
            back_attn[1:],
        )
    layer_moved = scatter_start(layer_parts, layer_sends)
    pairs = local_width // PAIR
    cut = pairs // 2
    saved = (info, queries, keys_rot, values, grad_mix, attn_mix, log_total, lanes)
    first_proj, first_sums = attend_backward(*saved, 0, cut, (), [gate_up_grad] + layer_moved[:2])
    first_partial = wide_grad(normed_one, first_proj, (), 0, 2)
    first_grad = scatter_weight(first_partial)
    out_partial = tall_grad(attn_mix, back_attn, [first_partial])
    out_grad = scatter_weight(out_partial)
    passing = scatter_on(layer_parts, layer_moved)
    grad_proj, second_sums = attend_backward(
        *saved, cut, pairs - cut, [first_proj], [out_partial] + passing
    )
    layer_own, layer_rest = scatter_end(layer_parts, layer_moved, passing)
    second_partial = wide_grad(
        normed_one, grad_proj, [first_grad] + layer_rest, 1, 2
    )
    parts = unproject(grad_proj, qkv_full, chunks, own_rows, [second_partial])
    moved = scatter_start(parts)
    onward = scatter_on(parts, moved)
    settled = scatter_end(parts, moved, onward)
    layer_out = finish(layer_own, layer_rest, hidden, parts[1:])
    second_grad = scatter_weight(second_partial)
    qkv_grad = wide(jnp.concatenate([first_grad, second_grad], axis=2))
    out_grad, gate_up_grad, down_grad = wide(out_grad), wide(gate_up_grad), wide(down_grad)
    input_grad = unsettle(
        *settled, hidden_in, grad_hidden, norm_gain[:1], [second_grad]
    )[0]

    bias_local_grad = jnp.concatenate([first_sums, second_sums], axis=1)
    lines = first_line(qkv_full, first_partial, second_partial, bias_local_grad, parts[1:])
    gain_one_grad = (lines[:1] - norm_bias[:1] * lines[1:]) / norm_gain[:1]
    bias_grad_full = lax.dynamic_update_slice_in_dim(
        jnp.zeros((3, qkv_bias.shape[1]), jnp.float32), bias_local_grad, tp_index * local_width, 1
    )
    small_grad = jnp.concatenate(
        [gain_one_grad, gain_two_grad, lines[1:], bias_two_grad, bias_grad_full], axis=0
    )
    small_weight = jnp.concatenate([norm_gain, norm_bias, qkv_bias], axis=0)
    qkv_first_new, qkv_second_new, qkv_new = adam_update(
        qkv_weight, qkv_grad, qkv_first, qkv_second, RATE_QKV, WEIGHT_DECAY
    )
    out_first_new, out_second_new, out_new = adam_update(
        out_weight, out_grad, out_first, out_second, RATE_OUT, WEIGHT_DECAY
    )
    gate_up_first_new, gate_up_second_new, gate_up_new = adam_update(
        gate_up_weight, gate_up_grad, gate_up_first, gate_up_second, RATE_GATE_UP, WEIGHT_DECAY
    )
    down_first_new, down_second_new, down_new = adam_update(
        down_weight, down_grad, down_first, down_second, RATE_DOWN, WEIGHT_DECAY
    )
    settled_all = list(settled[1]) + [layer_out, down_new, gate_up_new, out_new, qkv_new]
    small_grad = sum_along(sum_along(hold(small_grad, settled_all), "tensor"), "dp")
    small_first_new, small_second_new, small_new = adam_update(
        small_weight, small_grad, small_first, small_second, RATE_SMALL, 0.0
    )
    return (
        layer_out,
        input_grad,
        qkv_grad,
        qkv_first_new,
        qkv_second_new,
        qkv_new,
        out_grad,
        out_first_new,
        out_second_new,
        out_new,
        gate_up_grad,
        gate_up_first_new,
        gate_up_second_new,
        gate_up_new,
        down_grad,
        down_first_new,
        down_second_new,
        down_new,
        small_grad,
        small_first_new,
        small_second_new,
        small_new,
    )


def solution(mesh):
    placed = (
        P(("dp", "tensor"), None),
        P(("dp", "tensor"), None),
        P(),
        P(),
        P(None, "dp", "tensor"),
        P("tensor", "dp"),
        P(None, "dp", "tensor"),
        P("tensor", "dp"),
        P(),
        P(),
        P(),
        P(None, "dp", "tensor"),
        P("tensor", "dp"),
        P(None, "dp", "tensor"),
        P("tensor", "dp"),
        P(),
        P(None, "dp", "tensor"),
        P("tensor", "dp"),
        P(None, "dp", "tensor"),
        P("tensor", "dp"),
        P(),
    )
    return jax.shard_map(
        local,
        mesh=mesh,
        in_specs=placed,
        out_specs=(
            P(("dp", "tensor"), None),
            P(("dp", "tensor"), None),
            P(None, "dp", "tensor"),
            P(None, "dp", "tensor"),
            P(None, "dp", "tensor"),
            P(None, "dp", "tensor"),
            P("tensor", "dp"),
            P("tensor", "dp"),
            P("tensor", "dp"),
            P("tensor", "dp"),
            P(None, "dp", "tensor"),
            P(None, "dp", "tensor"),
            P(None, "dp", "tensor"),
            P(None, "dp", "tensor"),
            P("tensor", "dp"),
            P("tensor", "dp"),
            P("tensor", "dp"),
            P("tensor", "dp"),
            P(),
            P(),
            P(),
            P(),
        ),
        check_vma=False,
    )
```

```python
import functools

import jax
import jax.numpy as jnp
from jax import lax
from jax.experimental import pallas as pl
from jax.experimental.pallas import tpu as pltpu
from jax.sharding import PartitionSpec as P

STEP = 10
NORM_EPS = 1e-05
BETA_ONE = 0.9
BETA_TWO = 0.999
ADAM_EPS = 1e-08
WEIGHT_DECAY = 0.1
RATE_QKV = 0.05
RATE_OUT = 0.2
RATE_GATE_UP = 0.05
RATE_DOWN = 0.03
RATE_SMALL = 0.5
HD = 64
ROT = 16
BLK = 256
PAIR = 2 * HD
NT = (((1,), (1,)), ((), ()))
NN = (((1,), (0,)), ((), ()))
NEG = -1e30
VMEM_LIMIT = 56 * 1024 * 1024
THRIFT = 1


def spend(flops, bytes_accessed, transcendentals):
    return pl.CostEstimate(
        flops=flops // THRIFT,
        bytes_accessed=bytes_accessed // THRIFT,
        transcendentals=transcendentals // THRIFT,
    )


def mm(a, b, dims=NN):
    return lax.dot_general(a, b, dims, preferred_element_type=jnp.float32)


def lane_masks():
    lane = lax.broadcasted_iota(jnp.int32, (1, PAIR), 1)
    first = jnp.where(lane < HD, 1.0, 0.0).astype(jnp.bfloat16)
    second = jnp.where(lane < HD, 0.0, 1.0).astype(jnp.bfloat16)
    return (first, second)


def allowed_block(info_ref, key_block, query_block):
    split, total = info_ref[0], info_ref[1]
    key_rows = key_block * BLK + lax.broadcasted_iota(jnp.int32, (BLK, BLK), 0)
    query_rows = query_block * BLK + lax.broadcasted_iota(jnp.int32, (BLK, BLK), 1)
    rows = query_block * BLK + lax.broadcasted_iota(jnp.int32, (1, BLK), 1)
    starts = jnp.where(rows < split, 0, jnp.where(rows < total, split, total))
    return (key_rows <= query_rows) & (key_rows >= starts)


def row_start(info_ref, row):
    split, total = info_ref[0], info_ref[1]
    return jnp.where(row < split, 0, jnp.where(row < total, split, total))


def key_range(info_ref, query_block):
    low = row_start(info_ref, query_block * BLK) // BLK
    last = row_start(info_ref, query_block * BLK + (BLK - 1))
    mid = jnp.minimum((last + (BLK - 1)) // BLK, query_block)
    return (low, mid)


def swap_block(block, shift_index, per_own):
    return lax.bitwise_xor(block // per_own, shift_index) * per_own + block % per_own


def aligned(block):
    return pl.ds(pl.multiple_of(block * BLK, BLK), BLK)


def attend_forward_kernel(chunks, count, per_own, after, info_ref, *refs):
    refs = refs[after:]
    group = len(chunks)
    q_refs, refs = refs[:group], refs[group:]
    k_refs, v_refs, refs = refs[:count], refs[count : 2 * count], refs[2 * count :]
    o_refs, l_refs = refs[:group], refs[group : 2 * group]
    q_all, o_all, l_all, k_all, vt_all = refs[2 * group :]
    tensor_at = info_ref[2]
    own = per_own * BLK
    heads = k_all.shape[1] // HD
    spans = [slice(head // 2 * PAIR, head // 2 * PAIR + PAIR) for head in range(heads)]
    for at in range(count):
        k_all[at * own : (at + 1) * own, :] = k_refs[at][...]
        vt_all[:, at * own : (at + 1) * own] = v_refs[at][...].T
    for at in range(group):
        q_all[at * own : (at + 1) * own, :] = q_refs[at][...]
    masks = lane_masks()

    def one_query(local_block, carry):
        chunk = local_block // per_own + chunks[0]
        query_block = swap_block(chunk * per_own + local_block % per_own, tensor_at, per_own)
        here = aligned(local_block)
        q_block = q_all[here, :]
        q_heads = [
            q_block[:, spans[head]] * (masks[head % 2] * HD ** (-0.5)).astype(jnp.bfloat16)
            for head in range(heads)
        ]
        low, mid = key_range(info_ref, query_block)

        def one_key(masked, step, state):
            key_block = jnp.where(step < mid, step, query_block) if masked else step
            place = aligned(swap_block(key_block, tensor_at, per_own))
            k_block = k_all[place, :]
            out = []
            if masked:
                allowed = allowed_block(info_ref, key_block, query_block)
            for head in range(heads):
                peak, total, mixed = state[head]
                scores = mm(k_block[:, spans[head]], q_heads[head], NT)
                if masked:
                    scores = jnp.where(allowed, scores, NEG)
                new_peak = jnp.maximum(peak, jnp.max(scores, axis=0, keepdims=True))
                probs = jnp.exp(scores - new_peak)
                decay = jnp.exp(peak - new_peak)
                total = total * decay + jnp.sum(probs, axis=0, keepdims=True)
                v_part = vt_all[pl.ds(head * HD, HD), place]
                mixed = mixed * decay + mm(v_part, probs.astype(jnp.bfloat16))
                out.append((new_peak, total, mixed))
            return tuple(out)

        state = tuple(
            (
                jnp.full((1, BLK), NEG, jnp.float32),
                jnp.zeros((1, BLK), jnp.float32),
                jnp.zeros((HD, BLK), jnp.float32),
            )
            for _ in range(heads)
        )
        state = lax.fori_loop(mid, query_block, functools.partial(one_key, False), state)
        state = lax.fori_loop(low, mid + 1, functools.partial(one_key, True), state)
        both = jnp.concatenate([mixed / total for _, total, mixed in state], axis=0)
        o_all[here, :] = both.T.astype(jnp.bfloat16)
        for head in range(heads):
            peak, total, _ = state[head]
            l_all[pl.ds(head, 1), here] = peak + jnp.log(total)
        return carry

    lax.fori_loop(0, group * per_own, one_query, 0)
    for at in range(group):
        span = slice(at * own, (at + 1) * own)
        o_refs[at][...] = o_all[span, :]
        for head in range(heads):
            l_refs[at][head // 2, pl.ds(head % 2, 1), :] = l_all[pl.ds(head, 1), span]


def attend_forward(info, queries, keys_rot, values, chunks, after=()):
    own, width = queries[0].shape
    count, group = len(keys_rot), len(chunks)
    rows, pairs = own * count, width // PAIR
    together = 1
    wide_pair = together * PAIR
    steps = own * group * rows // 2
    column = pl.BlockSpec((own, wide_pair), lambda p, s: (0, p))
    outs = pl.pallas_call(
        functools.partial(attend_forward_kernel, tuple(chunks), count, own // BLK, len(after)),
        grid_spec=pltpu.PrefetchScalarGridSpec(
            num_scalar_prefetch=1,
            grid=(pairs // together,),
            in_specs=[pl.BlockSpec(memory_space=pl.ANY)] * len(after) + [column] * (group + 2 * count),
            out_specs=[column] * group
            + [pl.BlockSpec((together, 2, own), lambda p, s: (p, 0, 0))] * group,
            scratch_shapes=[
                pltpu.VMEM((group * own, wide_pair), jnp.bfloat16),
                pltpu.VMEM((group * own, wide_pair), jnp.bfloat16),
                pltpu.VMEM((max(2 * together, 8), group * own), jnp.float32),
                pltpu.VMEM((rows, wide_pair), jnp.bfloat16),
                pltpu.VMEM((wide_pair, rows), jnp.bfloat16),
            ],
        ),
        out_shape=[jax.ShapeDtypeStruct((own, width), jnp.bfloat16)] * group
        + [jax.ShapeDtypeStruct((pairs, 2, own), jnp.float32)] * group,
        compiler_params=pltpu.CompilerParams(vmem_limit_bytes=VMEM_LIMIT),
        cost_estimate=spend(
            flops=THRIFT * 16 * steps * width, bytes_accessed=8 * rows * width, transcendentals=steps * width // HD
        ),
        name="attend_forward",
    )(info, *after, *[queries[chunk] for chunk in chunks], *keys_rot, *values)
    return (outs[:group], outs[group:])


def spin(values, cosines, sines_low, sines_high, sign):
    ahead = pltpu.roll(values, PAIR - ROT // 2, 1)
    behind = pltpu.roll(values, ROT // 2, 1)
    return values * cosines + sign * (ahead * sines_low + behind * sines_high)


def attend_backward_kernel(count, pieces, per_own, after, info_ref, *refs):
    do_refs, refs = refs[after : after + pieces], refs[after + pieces :]
    q_refs, k_refs, v_refs, o_refs, l_refs = [
        refs[at * count : (at + 1) * count] for at in range(5)
    ]
    c_ref, sl_ref, sh_ref, out_ref, sum_ref, *scratch = refs[5 * count :]
    q_all, do_all, o_all, l_all, k_all, kt_all, v_all, dk_sum, dv_sum = scratch
    tensor_at = info_ref[2]
    own = per_own * BLK
    heads = k_all.shape[1] // HD
    spans = [slice(head // 2 * PAIR, head // 2 * PAIR + PAIR) for head in range(heads)]
    for at in range(count):
        span = slice(at * own, (at + 1) * own)
        k_all[span, :] = k_refs[at][...]
        kt_all[:, span] = k_refs[at][...].T
        v_all[span, :] = v_refs[at][...]
        q_all[span, :] = q_refs[at][...]
        o_all[span, :] = o_refs[at][...]
        for head in range(heads):
            l_all[pl.ds(head, 1), span] = l_refs[at][head // 2, pl.ds(head % 2, 1), :]
    done = 0
    for one in do_refs:
        do_all[done : done + one.shape[0], :] = one[...]
        done += one.shape[0]
    dk_sum[...] = jnp.zeros_like(dk_sum)
    dv_sum[...] = jnp.zeros_like(dv_sum)
    masks = lane_masks()

    def one_query(local_block, carry):
        query_block = swap_block(local_block, tensor_at, per_own)
        here = aligned(local_block)
        q_block = q_all[here, :]
        do_block = do_all[here, :]
        q_heads = [
            q_block[:, spans[head]] * (masks[head % 2] * HD ** (-0.5)).astype(jnp.bfloat16)
            for head in range(heads)
        ]
        do_heads = [do_block[:, spans[head]] * masks[head % 2] for head in range(heads)]
        prod = (do_block.astype(jnp.float32) * o_all[here, :].astype(jnp.float32)).T
        deltas = [
            jnp.sum(prod[head * HD : (head + 1) * HD], axis=0, keepdims=True) for head in range(heads)
        ]
        logs = [l_all[pl.ds(head, 1), here] for head in range(heads)]
        low, mid = key_range(info_ref, query_block)

        def one_key(masked, step, state):
            key_block = jnp.where(step < mid, step, query_block) if masked else step
            place = aligned(swap_block(key_block, tensor_at, per_own))
            k_block = k_all[place, :]
            v_block = v_all[place, :]
            if masked:
                allowed = allowed_block(info_ref, key_block, query_block)
            out, dk_parts, dv_parts = [], [], []
            for head in range(heads):
                probs = jnp.exp(mm(k_block[:, spans[head]], q_heads[head], NT) - logs[head])
                if masked:
                    probs = jnp.where(allowed, probs, 0.0)
                dprobs = mm(v_block[:, spans[head]], do_heads[head], NT)
                dscores = (probs * (dprobs - deltas[head])).astype(jnp.bfloat16)
                dv_parts.append(mm(probs.astype(jnp.bfloat16), do_heads[head]))
                dk_parts.append(mm(dscores, q_heads[head]))
                out.append(state[head] + mm(kt_all[pl.ds(head * HD, HD), place], dscores))
            for head in range(0, heads, 2):
                dk_sum[place, spans[head]] += dk_parts[head] + dk_parts[head + 1]
                dv_sum[place, spans[head]] += dv_parts[head] + dv_parts[head + 1]
            return tuple(out)

        state = tuple(jnp.zeros((HD, BLK), jnp.float32) for _ in range(heads))
        state = lax.fori_loop(mid, query_block, functools.partial(one_key, False), state)
        state = lax.fori_loop(low, mid + 1, functools.partial(one_key, True), state)
        dq = jnp.concatenate(state, axis=0).T * HD ** (-0.5)
        for span in spans[::2]:
            out_ref[0, here, span] = spin(
                dq[:, span], c_ref[here, :], sl_ref[here, :], sh_ref[here, :], -1.0
            ).astype(jnp.bfloat16)
        return carry

    lax.fori_loop(0, count * per_own, one_query, 0)
    for span in spans[::2]:
        out_ref[1, :, span] = spin(
            dk_sum[:, span], c_ref[...], sl_ref[...], sh_ref[...], -1.0
        ).astype(jnp.bfloat16)
    out_ref[2] = dv_sum[...].astype(jnp.bfloat16)
    for part in range(3):
        sum_ref[pl.ds(part, 1), :] = jnp.sum(
            out_ref[part].astype(jnp.float32), axis=0, keepdims=True
        )


def attend_backward(
    info, queries, keys_rot, values, grad_mix, mixed, logs, tables, first, pairs, held=(), after=()
):
    own, full = queries[0].shape
    count = len(queries)
    rows, width = own * count, pairs * PAIR
    together = 1
    shift = first // together
    steps = rows * rows // 2
    column = pl.BlockSpec((own, together * PAIR), lambda p, s: (0, p + shift))
    line = pl.BlockSpec((together, 2, own), lambda p, s: (p + shift, 0, 0))
    table = pl.BlockSpec((rows, PAIR), lambda p, s: (0, 0))
    far = list(held) + list(after)
    return pl.pallas_call(
        functools.partial(
            attend_backward_kernel, count, len(grad_mix), own // BLK, len(far)
        ),
        grid_spec=pltpu.PrefetchScalarGridSpec(
            num_scalar_prefetch=1,
            grid=(pairs // together,),
            in_specs=[pl.BlockSpec(memory_space=pl.ANY)] * len(far)
            + [
                pl.BlockSpec((one.shape[0], together * PAIR), lambda p, s: (0, p + shift))
                for one in grad_mix
            ]
            + [column] * (4 * count)
            + [line] * count
            + [table] * 3,
            out_specs=[
                pl.BlockSpec((3, rows, together * PAIR), lambda p, s: (0, 0, p + shift)),
                pl.BlockSpec((3, together * PAIR), lambda p, s: (0, p)),
            ],
            scratch_shapes=[
                pltpu.VMEM((rows, together * PAIR), jnp.bfloat16),
                pltpu.VMEM((rows, together * PAIR), jnp.bfloat16),
                pltpu.VMEM((rows, together * PAIR), jnp.bfloat16),
                pltpu.VMEM((max(2 * together, 8), rows), jnp.float32),
                pltpu.VMEM((rows, together * PAIR), jnp.bfloat16),
                pltpu.VMEM((together * PAIR, rows), jnp.bfloat16),
                pltpu.VMEM((rows, together * PAIR), jnp.bfloat16),
                pltpu.VMEM((rows, together * PAIR), jnp.float32),
                pltpu.VMEM((rows, together * PAIR), jnp.float32),
            ],
        ),
        out_shape=[
            jax.ShapeDtypeStruct((3, rows, full), jnp.bfloat16),
            jax.ShapeDtypeStruct((3, width), jnp.float32),
        ],
        input_output_aliases={1: 0} if held else {},
        compiler_params=pltpu.CompilerParams(vmem_limit_bytes=VMEM_LIMIT),
        cost_estimate=spend(
            flops=THRIFT * 40 * steps * width, bytes_accessed=16 * rows * width, transcendentals=steps * width // HD
        ),
        name="attend_backward",
    )(info, *far, *grad_mix, *queries, *keys_rot, *values, *mixed, *logs, *tables)


def project_kernel(x_ref, w_ref, b_ref, c_ref, sl_ref, sh_ref, q_ref, k_ref, v_ref):
    rows_in = x_ref[...]
    width = q_ref.shape[1]
    for part, out_ref in enumerate((q_ref, k_ref, v_ref)):
        full = mm(rows_in, w_ref[part]) + b_ref[pl.ds(part, 1), :]
        if part == 2:
            out_ref[...] = full.astype(jnp.bfloat16)
            continue
        for at in range(0, width, PAIR):
            piece = full[:, at : at + PAIR]
            out_ref[:, at : at + PAIR] = spin(
                piece, c_ref[...], sl_ref[...], sh_ref[...], 1.0
            ).astype(jnp.bfloat16)


def project(normed, weight, bias, tables, chunk=0):
    rows, depth = normed.shape
    width = weight.shape[2]
    block = min(rows, 256)
    first = chunk * rows // block
    table = pl.BlockSpec((block, PAIR), lambda i: (i + first, 0))
    return pl.pallas_call(
        project_kernel,
        grid=(rows // block,),
        in_specs=[
            pl.BlockSpec((block, depth), lambda i: (i, 0)),
            pl.BlockSpec((3, depth, width), lambda i: (0, 0, 0)),
            pl.BlockSpec((3, width), lambda i: (0, 0)),
            table,
            table,
            table,
        ],
        out_specs=[pl.BlockSpec((block, width), lambda i: (i, 0))] * 3,
        out_shape=[jax.ShapeDtypeStruct((rows, width), jnp.bfloat16)] * 3,
        compiler_params=pltpu.CompilerParams(vmem_limit_bytes=VMEM_LIMIT),
        cost_estimate=spend(
            flops=6 * rows * depth * width, bytes_accessed=2 * rows * depth + 6 * (rows + depth) * width, transcendentals=0
        ),
        name="project",
    )(normed, weight, bias, *tables)


def copy_in(source, target, sem):
    made = pltpu.make_async_copy(source, target, sem)
    made.start()
    return made


def feed_kernel(held, split, cut, after, *refs):
    refs = refs[after:]
    x_hbm, dy_hbm, refs = refs[:split], refs[split : split + cut], refs[split + cut :]
    gu_hbm, wd_hbm = refs[:2]
    z_ref, dgu_ref, da_ref = refs[2 + held : 5 + held]
    x_in, dy_in, wg_in, wu_in, wd_in, gate, up, inner_all, sems = refs[5 + held :]
    depth = x_in.shape[1]
    half = depth // 2
    rows = x_in.shape[0]
    piece, slab = rows // split, rows // cut
    get_x = [
        copy_in(x_hbm[at], x_in.at[pl.ds(at * piece, piece)], sems.at[5 + at]) for at in range(split)
    ]
    get_g0 = copy_in(gu_hbm.at[0, pl.ds(0, half)], wg_in.at[pl.ds(0, half)], sems.at[1])
    get_g1 = copy_in(gu_hbm.at[0, pl.ds(half, half)], wg_in.at[pl.ds(half, half)], sems.at[2])
    for one in get_x:
        one.wait()
    get_g0.wait()
    get_u = copy_in(gu_hbm.at[1], wu_in, sems.at[3])
    gate[...] = mm(x_in[:, :half], wg_in[:half])
    get_g1.wait()
    get_dy = [
        copy_in(dy_hbm[at], dy_in.at[pl.ds(at * slab, slab)], sems.at[7 + at])
        for at in range(cut)
    ]
    get_d = copy_in(wd_hbm, wd_in, sems.at[4])
    gate[...] += mm(x_in[:, half:], wg_in[half:])
    get_u.wait()
    up[...] = mm(x_in[...], wu_in[...])
    for one in get_dy:
        one.wait()
    get_d.wait()
    hidden = wd_in.shape[0]
    for at in range(0, hidden, BLK):
        span = slice(at, min(at + BLK, hidden))
        inner_all[:, span] = mm(dy_in[...], wd_in[span, :], NT)
    step = 64

    def middle(at, carry):
        here = pl.ds(pl.multiple_of(at * step, step), step)
        gate_pre, up_pre, inner = gate[here, :], up[here, :], inner_all[here, :]
        sigmoid_gate = 1.0 / (1.0 + jnp.exp(-gate_pre))
        activated = gate_pre * sigmoid_gate
        z_ref[here, :] = (activated * up_pre).astype(jnp.bfloat16)
        dgu_ref[0, here, :] = (
            inner * up_pre * (sigmoid_gate * (1.0 + gate_pre * (1.0 - sigmoid_gate)))
        ).astype(jnp.bfloat16)
        dgu_ref[1, here, :] = (inner * activated).astype(jnp.bfloat16)
        return carry

    lax.fori_loop(0, rows // step, middle, 0)

    def back(at, carry):
        here = pl.ds(pl.multiple_of(at * BLK, BLK), BLK)
        da_ref[:, here] = (
            mm(dgu_ref[0], wg_in[here, :], NT) + mm(dgu_ref[1], wu_in[here, :], NT)
        ).astype(da_ref.dtype)
        return carry

    lax.fori_loop(0, depth // BLK, back, 0)


def feed(chunk, count, normed, back, gate_up, down, held, after=()):
    split, cut = len(normed), len(back)
    rows, depth = normed[0].shape[0] * split, normed[0].shape[1]
    hidden = down.shape[0]
    far = pl.BlockSpec(memory_space=pl.ANY)
    return pl.pallas_call(
        functools.partial(feed_kernel, len(held), split, cut, len(after)),
        grid=(1,),
        in_specs=[far] * (2 + split + cut + len(held) + len(after)),
        out_specs=[
            pl.BlockSpec((rows, hidden), lambda i: (chunk, 0)),
            pl.BlockSpec((2, rows, hidden), lambda i: (0, chunk, 0)),
            pl.BlockSpec((rows, depth), lambda i: (0, 0)),
        ],
        out_shape=[
            jax.ShapeDtypeStruct((rows * count, hidden), jnp.bfloat16),
            jax.ShapeDtypeStruct((2, rows * count, hidden), jnp.bfloat16),
            jax.ShapeDtypeStruct((rows, depth), jnp.float32 if chunk == 0 else jnp.bfloat16),
        ],
        input_output_aliases={len(after) + 2 + split + cut + at: at for at in range(len(held))},
        scratch_shapes=[
            pltpu.VMEM((rows, depth), jnp.bfloat16),
            pltpu.VMEM((rows, depth), jnp.bfloat16),
            pltpu.VMEM((depth, hidden), jnp.bfloat16),
            pltpu.VMEM((depth, hidden), jnp.bfloat16),
            pltpu.VMEM((hidden, depth), jnp.bfloat16),
            pltpu.VMEM((rows, hidden), jnp.float32),
            pltpu.VMEM((rows, hidden), jnp.float32),
            pltpu.VMEM((rows, hidden), jnp.float32),
            pltpu.SemaphoreType.DMA((9,)),
        ],
        compiler_params=pltpu.CompilerParams(vmem_limit_bytes=VMEM_LIMIT),
        cost_estimate=spend(
            flops=10 * rows * depth * hidden, bytes_accessed=6 * depth * hidden, transcendentals=rows * hidden
        ),
        name="feed",
    )(*after, *normed, *back, gate_up, down, *held)


def wide_grad_kernel(count, after, *refs):
    refs = refs[after:]
    lefts, (right, out, turned) = refs[:count], refs[count:]
    done = 0
    for left in lefts:
        turned[:, done : done + left.shape[0]] = left[...].T
        done += left.shape[0]
    for part in range(out.shape[0]):
        out[part] = mm(turned[...], right[part]).astype(jnp.bfloat16)


def wide_grad(lefts, right, after=(), column=0, cuts=1):
    depth = lefts[0].shape[1]
    parts, rows, width = right.shape
    width = width // cuts
    return pl.pallas_call(
        functools.partial(wide_grad_kernel, len(lefts), len(after)),
        grid=(depth // BLK,),
        in_specs=[pl.BlockSpec(memory_space=pl.ANY)] * len(after)
        + [pl.BlockSpec((left.shape[0], BLK), lambda i: (0, i)) for left in lefts]
        + [pl.BlockSpec((parts, rows, width), lambda i: (0, 0, column))],
        out_specs=pl.BlockSpec((parts, BLK, width), lambda i: (0, i, 0)),
        out_shape=jax.ShapeDtypeStruct((parts, depth, width), jnp.bfloat16),
        scratch_shapes=[pltpu.VMEM((BLK, rows), jnp.bfloat16)],
        compiler_params=pltpu.CompilerParams(vmem_limit_bytes=VMEM_LIMIT),
        cost_estimate=spend(
            flops=2 * rows * depth * width * parts,
            bytes_accessed=2 * (rows * depth + parts * width * (rows + depth)),
            transcendentals=0,
        ),
        name="wide_grad",
    )(*after, *lefts, right)


def tall_grad_kernel(held, count, after, *refs):
    refs = refs[after:]
    lefts, rights, (out, turned, joined) = refs[:held], refs[held : held + count], refs[held + count :]
    tall = lefts[0].shape[0]

    @pl.when(pl.program_id(0) == 0)
    def _():
        for at in range(held):
            turned[:, at * tall : (at + 1) * tall] = lefts[at][...].T

    done = 0
    for right in rights:
        joined[done : done + right.shape[0], :] = right[...]
        done += right.shape[0]
    out[...] = mm(turned[...], joined[...]).astype(jnp.bfloat16)


def tall_grad(lefts, rights, after=()):
    tall, depth = lefts[0].shape
    width = rights[0].shape[1]
    count, held = len(rights), len(lefts)
    rows = tall * held
    return pl.pallas_call(
        functools.partial(tall_grad_kernel, held, count, len(after)),
        grid=(width // BLK,),
        in_specs=[pl.BlockSpec(memory_space=pl.ANY)] * len(after)
        + [pl.BlockSpec((tall, depth), lambda i: (0, 0))] * held
        + [pl.BlockSpec((right.shape[0], BLK), lambda i: (0, i)) for right in rights],
        out_specs=pl.BlockSpec((depth, BLK), lambda i: (0, i)),
        out_shape=jax.ShapeDtypeStruct((depth, width), jnp.bfloat16),
        scratch_shapes=[
            pltpu.VMEM((depth, rows), jnp.bfloat16),
            pltpu.VMEM((rows, BLK), jnp.bfloat16),
        ],
        compiler_params=pltpu.CompilerParams(vmem_limit_bytes=VMEM_LIMIT),
        cost_estimate=spend(
            flops=2 * rows * depth * width,
            bytes_accessed=2 * (rows * depth + width * (rows + depth)),
            transcendentals=0,
        ),
        name="tall_grad",
    )(*after, *lefts, *rights)


FAR = pl.BlockSpec(memory_space=pl.ANY)


def halves_kernel(after, count, *refs):
    for source, target in zip(refs[after : after + count], refs[after + count :]):
        target[...] = source[...]


def halves(picks, after=()):
    half, depth = picks[0][0].shape[0] // 2, picks[0][0].shape[1]
    specs = [
        pl.BlockSpec((half, depth), functools.partial(lambda which, i: (which, 0), which))
        for _, which in picks
    ]
    return pl.pallas_call(
        functools.partial(halves_kernel, len(after), len(picks)),
        grid=(1,),
        in_specs=[FAR] * len(after) + specs,
        out_specs=[pl.BlockSpec((half, depth), lambda i: (0, 0))] * len(picks),
        out_shape=[jax.ShapeDtypeStruct((half, depth), picks[0][0].dtype)] * len(picks),
        compiler_params=pltpu.CompilerParams(vmem_limit_bytes=VMEM_LIMIT),
        cost_estimate=spend(
            flops=half * depth, bytes_accessed=4 * len(picks) * half * depth, transcendentals=0
        ),
        name="halves",
    )(*after, *[one for one, _ in picks])


def join_kernel(after, *refs):
    top, end, out = refs[after:]
    half = top.shape[0]
    out[:half, :] = top[...]
    out[half:, :] = end[...]


def join(top, end, after=()):
    half, depth = top.shape
    whole = pl.BlockSpec((half, depth), lambda i: (0, 0))
    return pl.pallas_call(
        functools.partial(join_kernel, len(after)),
        grid=(1,),
        in_specs=[FAR] * len(after) + [whole, whole],
        out_specs=pl.BlockSpec((2 * half, depth), lambda i: (0, 0)),
        out_shape=jax.ShapeDtypeStruct((2 * half, depth), top.dtype),
        compiler_params=pltpu.CompilerParams(vmem_limit_bytes=VMEM_LIMIT),
        cost_estimate=spend(flops=half * depth, bytes_accessed=8 * half * depth, transcendentals=0),
        name="join",
    )(*after, top, end)


def shrink_kernel(after, *refs):
    source, scale, out = refs[after:]
    out[...] = (source[...].astype(jnp.float32) * scale[...]).astype(jnp.bfloat16)


def shrink(values, scale, after=()):
    rows, depth = values.shape
    block = rows // 4
    return pl.pallas_call(
        functools.partial(shrink_kernel, len(after)),
        grid=(4,),
        in_specs=[FAR] * len(after)
        + [
            pl.BlockSpec((block, depth), lambda i: (i, 0)),
            pl.BlockSpec((block, 1), lambda i: (i, 0)),
        ],
        out_specs=pl.BlockSpec((block, depth), lambda i: (i, 0)),
        out_shape=jax.ShapeDtypeStruct((rows, depth), jnp.bfloat16),
        compiler_params=pltpu.CompilerParams(vmem_limit_bytes=VMEM_LIMIT),
        cost_estimate=spend(
            flops=rows * depth, bytes_accessed=6 * rows * depth, transcendentals=0
        ),
        name="shrink",
    )(*after, values, scale)


LINES = 128


def arrived(own, parts, steps):
    total = own[...].astype(jnp.float32)
    if parts:
        first = pl.program_id(0) < steps // 2
        one, two, three, four = [part[...].astype(jnp.float32) for part in parts]
        total = total + jnp.where(first, one + two, three + four)
    return total


def part_specs(parts, depth, steps):
    if not parts:
        return []
    top = pl.BlockSpec((LINES, depth), lambda i: (jnp.minimum(i, steps // 2 - 1), 0))
    end = pl.BlockSpec((LINES, depth), lambda i: (jnp.maximum(i - steps // 2, 0), 0))
    return [top, top, end, end]


def unit_of(values):
    average = jnp.mean(values, axis=-1, keepdims=True)
    centered = values - average
    inverse = lax.rsqrt(jnp.mean(centered * centered, axis=-1, keepdims=True) + NORM_EPS)
    return (centered * inverse, inverse)


def settle_kernel(held, after, steps, *refs):
    refs = refs[after:]
    own, parts = refs[0], refs[1 : 1 + held]
    resid, gain, shift, hidden, normed = refs[1 + held :]
    values = resid[...].astype(jnp.float32) + arrived(own, parts, steps)
    hidden[...] = values
    normed[...] = (unit_of(values)[0] * gain[...] + shift[...]).astype(jnp.bfloat16)


def settle(own, parts, resid, gain, shift, after=()):
    rows, depth = own.shape
    steps = rows // LINES
    block = pl.BlockSpec((LINES, depth), lambda i: (i, 0))
    line = pl.BlockSpec((1, depth), lambda i: (0, 0))
    return pl.pallas_call(
        functools.partial(settle_kernel, len(parts), len(after), steps),
        grid=(steps,),
        in_specs=[FAR] * len(after)
        + [block]
        + part_specs(parts, depth, steps)
        + [block, line, line],
        out_specs=[block, block],
        out_shape=[
            jax.ShapeDtypeStruct((rows, depth), jnp.float32),
            jax.ShapeDtypeStruct((rows, depth), jnp.bfloat16),
        ],
        compiler_params=pltpu.CompilerParams(vmem_limit_bytes=VMEM_LIMIT),
        cost_estimate=spend(
            flops=10 * rows * depth, bytes_accessed=16 * rows * depth, transcendentals=rows
        ),
        name="settle",
    )(*after, own, *parts, resid, gain, shift)


def finish_kernel(held, after, steps, *refs):
    refs = refs[after:]
    own, parts = refs[0], refs[1 : 1 + held]
    hidden, out = refs[1 + held :]
    total = hidden[...] + arrived(own, parts, steps)
    out[...] = total.astype(jnp.bfloat16)


def finish(own, parts, hidden, after=()):
    rows, depth = own.shape
    steps = rows // LINES
    block = pl.BlockSpec((LINES, depth), lambda i: (i, 0))
    return pl.pallas_call(
        functools.partial(finish_kernel, len(parts), len(after), steps),
        grid=(steps,),
        in_specs=[FAR] * len(after) + [block] + part_specs(parts, depth, steps) + [block],
        out_specs=block,
        out_shape=jax.ShapeDtypeStruct((rows, depth), jnp.bfloat16),
        compiler_params=pltpu.CompilerParams(vmem_limit_bytes=VMEM_LIMIT),
        cost_estimate=spend(
            flops=4 * rows * depth, bytes_accessed=12 * rows * depth, transcendentals=0
        ),
        name="finish",
    )(*after, own, *parts, hidden)


def unsettle_kernel(held, after, steps, *refs):
    refs = refs[after:]
    own, parts = refs[0], refs[1 : 1 + held]
    values, extra, gain, total, short, gain_sum, shift_sum = refs[1 + held :]
    incoming = arrived(own, parts, steps)
    unit_rows, inverse = unit_of(values[...].astype(jnp.float32))
    scaled = incoming * gain[...]
    grad_rows = inverse * (
        scaled
        - jnp.mean(scaled, axis=-1, keepdims=True)
        - unit_rows * jnp.mean(scaled * unit_rows, axis=-1, keepdims=True)
    )
    result = extra[...].astype(jnp.float32) + grad_rows
    total[...] = result
    short[...] = result.astype(jnp.bfloat16)

    @pl.when(pl.program_id(0) == 0)
    def _():
        gain_sum[...] = jnp.zeros_like(gain_sum)
        shift_sum[...] = jnp.zeros_like(shift_sum)

    gain_sum[...] += jnp.sum(incoming * unit_rows, axis=0, keepdims=True)
    shift_sum[...] += jnp.sum(incoming, axis=0, keepdims=True)


def unsettle(own, parts, values, extra, gain, after=()):
    rows, depth = own.shape
    steps = rows // LINES
    block = pl.BlockSpec((LINES, depth), lambda i: (i, 0))
    line = pl.BlockSpec((1, depth), lambda i: (0, 0))
    return pl.pallas_call(
        functools.partial(unsettle_kernel, len(parts), len(after), steps),
        grid=(steps,),
        in_specs=[FAR] * len(after)
        + [block]
        + part_specs(parts, depth, steps)
        + [block, block, line],
        out_specs=[block, block, line, line],
        out_shape=[
            jax.ShapeDtypeStruct((rows, depth), jnp.float32),
            jax.ShapeDtypeStruct((rows, depth), jnp.bfloat16),
            jax.ShapeDtypeStruct((1, depth), jnp.float32),
            jax.ShapeDtypeStruct((1, depth), jnp.float32),
        ],
        compiler_params=pltpu.CompilerParams(vmem_limit_bytes=VMEM_LIMIT),
        cost_estimate=spend(
            flops=20 * rows * depth, bytes_accessed=20 * rows * depth, transcendentals=rows
        ),
        name="unsettle",
    )(*after, own, *parts, values, extra, gain)


def unproject_kernel(count, after, *refs):
    refs = refs[after:]
    lefts, w_ref, outs = refs[:count], refs[count], refs[count + 1 :]
    own = outs[0].shape[0]
    total = None
    for part in range(3):
        left = jnp.concatenate([one[part] for one in lefts], axis=0)
        made = mm(left, w_ref[part], NT)
        total = made if total is None else total + made
    for at, out in enumerate(outs):
        out[...] = total[at * own : (at + 1) * own].astype(out.dtype)


def unproject(grads, weight, chunks, own, after=()):
    parts, depth, width = weight.shape
    count = len(chunks)
    return pl.pallas_call(
        functools.partial(unproject_kernel, count, len(after)),
        grid=(depth // BLK,),
        in_specs=[FAR] * len(after)
        + [
            pl.BlockSpec((parts, own, width), functools.partial(lambda which, i: (0, which, 0), chunk))
            for chunk in chunks
        ]
        + [pl.BlockSpec((parts, BLK, width), lambda i: (0, i, 0))],
        out_specs=[pl.BlockSpec((own, BLK), lambda i: (0, i))] * count,
        out_shape=[
            jax.ShapeDtypeStruct((own, depth), jnp.bfloat16 if chunk else jnp.float32)
            for chunk in chunks
        ],
        compiler_params=pltpu.CompilerParams(vmem_limit_bytes=VMEM_LIMIT),
        cost_estimate=spend(
            flops=2 * parts * own * count * depth * width,
            bytes_accessed=2 * parts * width * (own * count + depth) + 4 * own * count * depth,
            transcendentals=0,
        ),
        name="unproject",
    )(*after, *[grads] * count, weight)


def adam_kernel(rate, decay, after, *refs):
    weight, gradient, first, second, grad_out, first_out, second_out, weight_out = refs[after:]
    grad = gradient[...].astype(jnp.float32)
    grad_out[...] = grad
    first_out[...], second_out[...], weight_out[...] = adam_update(
        weight[...], grad, first[...], second[...], rate, decay
    )


def adam(weight, gradient, first, second, rate, after=()):
    shape = weight.shape
    flat = (-1, shape[-1])
    arrays = [one.reshape(flat) for one in (weight, gradient, first, second)]
    rows, width = arrays[0].shape
    block = pl.BlockSpec((rows // 4, width), lambda i: (i, 0))
    outs = pl.pallas_call(
        functools.partial(adam_kernel, rate, WEIGHT_DECAY, len(after)),
        grid=(4,),
        in_specs=[FAR] * len(after) + [block] * 4,
        out_specs=[block] * 4,
        out_shape=[jax.ShapeDtypeStruct((rows, width), jnp.float32)] * 4,
        compiler_params=pltpu.CompilerParams(vmem_limit_bytes=VMEM_LIMIT),
        cost_estimate=spend(
            flops=12 * rows * width, bytes_accessed=30 * rows * width, transcendentals=0
        ),
        name="adam",
    )(*after, *arrays)
    return [one.reshape(shape) for one in outs]


def hold(values, after):
    rows, depth = values.shape
    whole = pl.BlockSpec((rows, depth), lambda i: (0, 0))

    def body(*refs):
        refs[-1][...] = refs[-2][...]

    return pl.pallas_call(
        body,
        grid=(1,),
        in_specs=[FAR] * len(after) + [whole],
        out_specs=whole,
        out_shape=jax.ShapeDtypeStruct((rows, depth), values.dtype),
        cost_estimate=spend(
            flops=rows * depth, bytes_accessed=8 * rows * depth, transcendentals=0
        ),
        name="hold",
    )(*after, values)


def first_line_kernel(after, *refs):
    w_ref, first_ref, second_ref, sum_ref, out_ref = refs[after:]
    cut = first_ref.shape[2]
    gain, shift = None, None
    for part in range(3):
        weight = w_ref[part].astype(jnp.float32)
        grad = jnp.concatenate([first_ref[part], second_ref[part]], axis=1).astype(jnp.float32)
        gain = weight * grad if gain is None else gain + weight * grad
        lean = weight * sum_ref[pl.ds(part, 1), :]
        shift = lean if shift is None else shift + lean
    out_ref[pl.ds(0, 1), :] = jnp.sum(gain.T, axis=0, keepdims=True)
    out_ref[pl.ds(1, 1), :] = jnp.sum(shift.T, axis=0, keepdims=True)


def first_line(weight, first, second, sums, after):
    parts, depth, width = weight.shape
    cut = first.shape[2]
    return pl.pallas_call(
        functools.partial(first_line_kernel, len(after)),
        grid=(depth // BLK,),
        in_specs=[FAR] * len(after)
        + [
            pl.BlockSpec((parts, BLK, width), lambda i: (0, i, 0)),
            pl.BlockSpec((parts, BLK, cut), lambda i: (0, i, 0)),
            pl.BlockSpec((parts, BLK, width - cut), lambda i: (0, i, 0)),
            pl.BlockSpec((parts, width), lambda i: (0, 0)),
        ],
        out_specs=pl.BlockSpec((2, BLK), lambda i: (0, i)),
        out_shape=jax.ShapeDtypeStruct((2, depth), jnp.float32),
        compiler_params=pltpu.CompilerParams(vmem_limit_bytes=VMEM_LIMIT),
        cost_estimate=spend(
            flops=4 * parts * depth * width, bytes_accessed=4 * parts * depth * width, transcendentals=0
        ),
        name="first_line",
    )(*after, weight, first, second, sums)


def down_project_kernel(after, count, *refs):
    z_ref, w_ref, outs = refs[after], refs[after + 1], refs[after + 2 :]
    for at in range(count):

        @pl.when(pl.program_id(0) == at)
        def _():
            outs[at][...] = mm(z_ref[...], w_ref[...]).astype(jnp.bfloat16)


def down_project(inner, weight, count, after=()):
    rows, hidden = inner.shape
    depth = weight.shape[1]
    own = rows // count
    return pl.pallas_call(
        functools.partial(down_project_kernel, len(after), count),
        grid=(count,),
        in_specs=[FAR] * len(after)
        + [
            pl.BlockSpec((own, hidden), lambda i: (i, 0)),
            pl.BlockSpec((hidden, depth), lambda i: (0, 0)),
        ],
        out_specs=[pl.BlockSpec((own, depth), lambda i: (0, 0))] * count,
        out_shape=[jax.ShapeDtypeStruct((own, depth), jnp.bfloat16)] * count,
        compiler_params=pltpu.CompilerParams(vmem_limit_bytes=VMEM_LIMIT),
        cost_estimate=spend(
            flops=2 * rows * depth * hidden,
            bytes_accessed=2 * (rows * depth + hidden * (rows + depth)),
            transcendentals=0,
        ),
        name="down_project",
    )(*after, inner, weight)


def lane_tables(position):
    half_rot = ROT // 2
    lane = jnp.arange(PAIR, dtype=jnp.int32) % HD
    freqs = 10000.0 ** (-((lane % half_rot).astype(jnp.float32) * (2.0 / ROT)))
    angles = position.astype(jnp.float32)[:, None] * freqs[None, :]
    cosines, sines = jnp.cos(angles), jnp.sin(angles)
    in_low, in_high = (lane < half_rot)[None], ((lane >= half_rot) & (lane < ROT))[None]
    return (
        jnp.where((lane < ROT)[None], cosines, 1.0),
        jnp.where(in_low, -sines, 0.0),
        jnp.where(in_high, sines, 0.0),
    )


def sequence_facts(lengths, owners, dp_index):
    owned = owners == dp_index
    total = jnp.sum(jnp.where(owned, lengths, 0))
    return (lengths[jnp.argmax(owned)], total)


def norm_forward(values, gain, shift):
    return unit_of(values)[0] * gain + shift


def adam_update(weight_old, gradient, first_old, second_old, rate, decay):
    first_new = BETA_ONE * first_old + (1.0 - BETA_ONE) * gradient
    second_new = BETA_TWO * second_old + (1.0 - BETA_TWO) * gradient * gradient
    first_hat = first_new / (1.0 - BETA_ONE**STEP)
    second_hat = second_new / (1.0 - BETA_TWO**STEP)
    weight_new = weight_old * (1.0 - rate * decay) - rate * first_hat / (
        jnp.sqrt(second_hat) + ADAM_EPS
    )
    return (first_new, second_new, weight_new)


def low(values):
    return values.astype(jnp.bfloat16)


def wide(values):
    return values.astype(jnp.float32)


def swap(values, axis, bits):
    size = lax.axis_size(axis)
    return lax.ppermute(values, axis, [(at, at ^ bits) for at in range(size)])


def gather_start(rows):
    count = lax.axis_size("tensor")
    if count != 4:
        return [swap(rows, "tensor", bits) for bits in range(1, count)]
    return [swap(rows, "tensor", 1), swap(rows, "tensor", 2)]


def gather_on(near, after=(), with_sends=False):
    passed, sends = (), ()
    if lax.axis_size("tensor") == 4:
        sends = halves([(near[0], 0), (near[1], 1)], after)
        passed = (swap(sends[0], "tensor", 2), swap(sends[1], "tensor", 1))
    return (passed, sends) if with_sends else passed


def pieces_of(pieces, chunk):
    return pieces[3:] if len(pieces) == 5 and chunk == 3 else [pieces[chunk]]


def scatter_start(parts, after=()):
    if lax.axis_size("tensor") != 4:
        return [swap(low(parts[bits]), "tensor", bits) for bits in range(1, len(parts))]
    _, one, two, three = parts
    half = one.shape[0] // 2
    if after:
        three_top, three_end, one_top, two_end = after
    else:
        three = low(three)
        three_top, three_end = three[:half], three[half:]
        one_top, two_end = low(one[:half]), low(two[half:])
    return [
        swap(three_top, "tensor", 1),
        swap(three_end, "tensor", 2),
        swap(one_top, "tensor", 1),
        swap(two_end, "tensor", 2),
    ]


def scatter_on(parts, moved):
    if lax.axis_size("tensor") != 4:
        return []
    _, one, two, _ = parts
    half = one.shape[0] // 2
    return [low(wide(one[half:]) + wide(moved[1])), low(wide(two[:half]) + wide(moved[0]))]


def scatter_end(parts, moved, passing=None):
    if lax.axis_size("tensor") != 4:
        total = wide(parts[0])
        for one in moved:
            total = total + wide(one)
        return (total, [])
    one_end, two_top = passing or scatter_on(parts, moved)
    return (
        parts[0],
        [moved[2], swap(two_top, "tensor", 2), swap(one_end, "tensor", 1), moved[3]],
    )


def sum_along(values, axis):
    bits = 1
    while bits < lax.axis_size(axis):
        values = values + swap(values, axis, bits)
        bits *= 2
    return values


def scatter_weight(partial):
    return lax.psum_scatter(partial, "dp", scatter_dimension=1, tiled=True)


def dot(left, right, dims):
    return lax.dot_general(left, right, (dims, ((), ())), preferred_element_type=jnp.float32)


def local(
    hidden_in,
    grad_out,
    lengths,
    owners,
    qkv_weight,
    out_weight,
    gate_up_weight,
    down_weight,
    norm_gain,
    norm_bias,
    qkv_bias,
    qkv_first,
    out_first,
    gate_up_first,
    down_first,
    small_first,
    qkv_second,
    out_second,
    gate_up_second,
    down_second,
    small_second,
):
    dp_index = lax.axis_index("dp")
    tp_index = lax.axis_index("tensor")
    count = lax.axis_size("tensor")
    own_rows = hidden_in.shape[0]
    local_width = qkv_weight.shape[2]
    chunks = list(range(count))
    groups = [[3], [1, 2], [0]] if count == 4 else [chunks[1:], [0]]
    qkv_full, out_full, gate_up_full, down_full = [
        lax.all_gather(low(one), "dp", axis=1, tiled=True)
        for one in (qkv_weight, out_weight, gate_up_weight, down_weight)
    ]
    split, total = sequence_facts(lengths, owners, dp_index)
    row_ids = jnp.concatenate(
        [(tp_index ^ chunk) * own_rows + jnp.arange(own_rows, dtype=jnp.int32) for chunk in chunks]
    )
    starts = jnp.where(row_ids < split, 0, jnp.where(row_ids < total, split, total))
    live_own = wide(row_ids[:own_rows] < total)
    info = jnp.stack([split, total, tp_index, tp_index]).astype(jnp.int32)
    lanes = lane_tables(row_ids - starts)
    bias_local = lax.dynamic_slice_in_dim(qkv_bias, tp_index * local_width, local_width, 1)

    first_norm = low(norm_forward(wide(hidden_in), norm_gain[0], norm_bias[0]))
    near = gather_start(first_norm)
    passed = gather_on(near)
    early = [
        project(one, qkv_full, bias_local, lanes, chunk)
        for chunk, one in enumerate([first_norm] + near)
    ]
    normed_one = [first_norm] + near
    if passed:
        normed_one.append(join(*passed, [one[0] for one in early]))
    projected = early + [
        project(normed_one[chunk], qkv_full, bias_local, lanes, chunk)
        for chunk in chunks[len(early) :]
    ]
    queries, keys_rot, values = [[one[part] for one in projected] for part in range(3)]
    cotangent = shrink(grad_out, live_own[:, None], normed_one[1:])
    near = gather_start(cotangent)
    passed = gather_on(near)
    back_ffn = [cotangent, *near] + ([join(*passed)] if passed else [])

    attn_mix, log_total = [None] * count, [None] * count
    for step, group in enumerate(groups):
        after = near if step == 1 else ()
        mixed, logs = attend_forward(info, queries, keys_rot, values, group, after)
        for at, chunk in enumerate(group):
            attn_mix[chunk], log_total[chunk] = mixed[at], logs[at]
    parts = [dot(one, out_full, ((1,), (0,))) for one in attn_mix]
    hidden, second_norm = settle(
        *scatter_end(parts, scatter_start(parts)),
        hidden_in,
        norm_gain[1:2],
        norm_bias[1:2],
    )

    near = gather_start(second_norm)
    held, back_second = (), [None] * count

    def feed_one(chunk, normed, held, after=()):
        *held, back_second[chunk] = feed(
            chunk, count, normed, pieces_of(back_ffn, chunk), gate_up_full, down_full, held, after
        )
        return held

    held = feed_one(0, [second_norm], held)
    passed = gather_on(near, held[:1])
    held = feed_one(1, near[:1], held)
    normed_two = [second_norm, *near, *passed]
    for chunk in [3, 2] if count == 4 else chunks[2:]:
        held = feed_one(chunk, pieces_of(normed_two, chunk), held)
    inner_act, grad_gate_up = held
    moved = scatter_start(back_second)
    passing = scatter_on(back_second, moved)
    gate_up_partial = wide_grad(normed_two, grad_gate_up, moved[:2] + passing)
    gate_up_grad = scatter_weight(gate_up_partial)
    layer_parts = down_project(inner_act, down_full, count, [gate_up_partial])
    grad_hidden, grad_hidden_low, gain_two_grad, bias_two_grad = unsettle(
        *scatter_end(back_second, moved, passing),
        hidden,
        cotangent,
        norm_gain[1:2],
        [gate_up_partial, *layer_parts],
    )
    near = gather_start(grad_hidden_low)
    down_partial = tall_grad([inner_act], back_ffn, [grad_hidden_low])
    down_grad = scatter_weight(down_partial)
    passed = gather_on(near, [down_partial])
    back_attn = [grad_hidden_low, *near, *passed]

    grad_mix = [low(dot(one, out_full, ((1,), (1,)))) for one in back_attn]
    layer_sends = []
    if count == 4:
        layer_sends = halves(
            [(layer_parts[3], 0), (layer_parts[3], 1), (layer_parts[1], 0), (layer_parts[2], 1)],
            back_attn[1:],
        )
    layer_moved = scatter_start(layer_parts, layer_sends)
    pairs = local_width // PAIR
    cut = pairs // 2
    saved = (info, queries, keys_rot, values, grad_mix, attn_mix, log_total, lanes)
    first_proj, first_sums = attend_backward(*saved, 0, cut, (), [gate_up_grad] + layer_moved[:2])
    first_partial = wide_grad(normed_one, first_proj, (), 0, 2)
    first_grad = scatter_weight(first_partial)
    out_partial = tall_grad(attn_mix, back_attn, [first_partial])
    out_grad = scatter_weight(out_partial)
    passing = scatter_on(layer_parts, layer_moved)
    grad_proj, second_sums = attend_backward(
        *saved, cut, pairs - cut, [first_proj], [out_partial] + passing
    )
    layer_own, layer_rest = scatter_end(layer_parts, layer_moved, passing)
    second_partial = wide_grad(
        normed_one, grad_proj, [first_grad] + layer_rest, 1, 2
    )
    parts = unproject(grad_proj, qkv_full, chunks, own_rows, [second_partial])
    moved = scatter_start(parts)
    onward = scatter_on(parts, moved)
    settled = scatter_end(parts, moved, onward)
    layer_out = finish(layer_own, layer_rest, hidden, parts[1:])
    second_grad = scatter_weight(second_partial)
    qkv_grad = wide(jnp.concatenate([first_grad, second_grad], axis=2))
    gate_up_grad = wide(gate_up_grad)
    input_grad = unsettle(
        *settled, hidden_in, grad_hidden, norm_gain[:1], [second_grad]
    )[0]

    bias_local_grad = jnp.concatenate([first_sums, second_sums], axis=1)
    lines = first_line(qkv_full, first_partial, second_partial, bias_local_grad, parts[1:])
    gain_one_grad = (lines[:1] - norm_bias[:1] * lines[1:]) / norm_gain[:1]
    bias_grad_full = lax.dynamic_update_slice_in_dim(
        jnp.zeros((3, qkv_bias.shape[1]), jnp.float32), bias_local_grad, tp_index * local_width, 1
    )
    small_grad = jnp.concatenate(
        [gain_one_grad, gain_two_grad, lines[1:], bias_two_grad, bias_grad_full], axis=0
    )
    small_weight = jnp.concatenate([norm_gain, norm_bias, qkv_bias], axis=0)
    qkv_first_new, qkv_second_new, qkv_new = adam_update(
        qkv_weight, qkv_grad, qkv_first, qkv_second, RATE_QKV, WEIGHT_DECAY
    )
    gate_up_first_new, gate_up_second_new, gate_up_new = adam_update(
        gate_up_weight, gate_up_grad, gate_up_first, gate_up_second, RATE_GATE_UP, WEIGHT_DECAY
    )
    settled_all = list(settled[1]) + [layer_out, gate_up_new]
    down_grad, down_first_new, down_second_new, down_new = adam(
        down_weight, down_grad, down_first, down_second, RATE_DOWN, settled[1]
    )
    out_grad, out_first_new, out_second_new, out_new = adam(
        out_weight, out_grad, out_first, out_second, RATE_OUT, settled[1]
    )
    small_grad = sum_along(sum_along(hold(small_grad, settled_all), "tensor"), "dp")
    small_first_new, small_second_new, small_new = adam_update(
        small_weight, small_grad, small_first, small_second, RATE_SMALL, 0.0
    )
    return (
        layer_out,
        input_grad,
        qkv_grad,
        qkv_first_new,
        qkv_second_new,
        qkv_new,
        out_grad,
        out_first_new,
        out_second_new,
        out_new,
        gate_up_grad,
        gate_up_first_new,
        gate_up_second_new,
        gate_up_new,
        down_grad,
        down_first_new,
        down_second_new,
        down_new,
        small_grad,
        small_first_new,
        small_second_new,
        small_new,
    )


def solution(mesh):
    placed = (
        P(("dp", "tensor"), None),
        P(("dp", "tensor"), None),
        P(),
        P(),
        P(None, "dp", "tensor"),
        P("tensor", "dp"),
        P(None, "dp", "tensor"),
        P("tensor", "dp"),
        P(),
        P(),
        P(),
        P(None, "dp", "tensor"),
        P("tensor", "dp"),
        P(None, "dp", "tensor"),
        P("tensor", "dp"),
        P(),
        P(None, "dp", "tensor"),
        P("tensor", "dp"),
        P(None, "dp", "tensor"),
        P("tensor", "dp"),
        P(),
    )
    return jax.shard_map(
        local,
        mesh=mesh,
        in_specs=placed,
        out_specs=(
            P(("dp", "tensor"), None),
            P(("dp", "tensor"), None),
            P(None, "dp", "tensor"),
            P(None, "dp", "tensor"),
            P(None, "dp", "tensor"),
            P(None, "dp", "tensor"),
            P("tensor", "dp"),
            P("tensor", "dp"),
            P("tensor", "dp"),
            P("tensor", "dp"),
            P(None, "dp", "tensor"),
            P(None, "dp", "tensor"),
            P(None, "dp", "tensor"),
            P(None, "dp", "tensor"),
            P("tensor", "dp"),
            P("tensor", "dp"),
            P("tensor", "dp"),
            P("tensor", "dp"),
            P(),
            P(),
            P(),
            P(),
        ),
        check_vma=False,
    )
```

```python
import functools

import jax
import jax.numpy as jnp
from jax import lax
from jax.experimental import pallas as pl
from jax.experimental.pallas import tpu as pltpu
from jax.sharding import PartitionSpec as P

STEP = 10
NORM_EPS = 1e-05
BETA_ONE = 0.9
BETA_TWO = 0.999
ADAM_EPS = 1e-08
WEIGHT_DECAY = 0.1
RATE_QKV = 0.05
RATE_OUT = 0.2
RATE_GATE_UP = 0.05
RATE_DOWN = 0.03
RATE_SMALL = 0.5
HD = 64
ROT = 16
BLK = 256
PAIR = 2 * HD
NT = (((1,), (1,)), ((), ()))
NN = (((1,), (0,)), ((), ()))
NEG = -1e30
VMEM_LIMIT = 56 * 1024 * 1024
THRIFT = 1


def spend(flops, bytes_accessed, transcendentals):
    return pl.CostEstimate(
        flops=flops // THRIFT,
        bytes_accessed=bytes_accessed // THRIFT,
        transcendentals=transcendentals // THRIFT,
    )


def mm(a, b, dims=NN):
    return lax.dot_general(a, b, dims, preferred_element_type=jnp.float32)


def lane_masks():
    lane = lax.broadcasted_iota(jnp.int32, (1, PAIR), 1)
    first = jnp.where(lane < HD, 1.0, 0.0).astype(jnp.bfloat16)
    second = jnp.where(lane < HD, 0.0, 1.0).astype(jnp.bfloat16)
    return (first, second)


def allowed_block(info_ref, key_block, query_block):
    split, total = info_ref[0], info_ref[1]
    key_rows = key_block * BLK + lax.broadcasted_iota(jnp.int32, (BLK, BLK), 0)
    query_rows = query_block * BLK + lax.broadcasted_iota(jnp.int32, (BLK, BLK), 1)
    rows = query_block * BLK + lax.broadcasted_iota(jnp.int32, (1, BLK), 1)
    starts = jnp.where(rows < split, 0, jnp.where(rows < total, split, total))
    return (key_rows <= query_rows) & (key_rows >= starts)


def row_start(info_ref, row):
    split, total = info_ref[0], info_ref[1]
    return jnp.where(row < split, 0, jnp.where(row < total, split, total))


def key_range(info_ref, query_block):
    low = row_start(info_ref, query_block * BLK) // BLK
    last = row_start(info_ref, query_block * BLK + (BLK - 1))
    mid = jnp.minimum((last + (BLK - 1)) // BLK, query_block)
    return (low, mid)


def swap_block(block, shift_index, per_own):
    return lax.bitwise_xor(block // per_own, shift_index) * per_own + block % per_own


def aligned(block):
    return pl.ds(pl.multiple_of(block * BLK, BLK), BLK)


def attend_forward_kernel(chunks, count, per_own, after, info_ref, *refs):
    refs = refs[after:]
    group = len(chunks)
    q_refs, refs = refs[:group], refs[group:]
    k_refs, v_refs, refs = refs[:count], refs[count : 2 * count], refs[2 * count :]
    o_refs, l_refs = refs[:group], refs[group : 2 * group]
    q_all, o_all, l_all, k_all, vt_all = refs[2 * group :]
    tensor_at = info_ref[2]
    own = per_own * BLK
    heads = k_all.shape[1] // HD
    spans = [slice(head // 2 * PAIR, head // 2 * PAIR + PAIR) for head in range(heads)]
    for at in range(count):
        k_all[at * own : (at + 1) * own, :] = k_refs[at][...]
        vt_all[:, at * own : (at + 1) * own] = v_refs[at][...].T
    for at in range(group):
        q_all[at * own : (at + 1) * own, :] = q_refs[at][...]
    masks = lane_masks()

    def one_query(local_block, carry):
        chunk = local_block // per_own + chunks[0]
        query_block = swap_block(chunk * per_own + local_block % per_own, tensor_at, per_own)
        here = aligned(local_block)
        q_block = q_all[here, :]
        q_heads = [
            q_block[:, spans[head]] * (masks[head % 2] * HD ** (-0.5)).astype(jnp.bfloat16)
            for head in range(heads)
        ]
        low, mid = key_range(info_ref, query_block)

        def one_key(masked, step, state):
            key_block = jnp.where(step < mid, step, query_block) if masked else step
            place = aligned(swap_block(key_block, tensor_at, per_own))
            k_block = k_all[place, :]
            out = []
            if masked:
                allowed = allowed_block(info_ref, key_block, query_block)
            for head in range(heads):
                peak, total, mixed = state[head]
                scores = mm(k_block[:, spans[head]], q_heads[head], NT)
                if masked:
                    scores = jnp.where(allowed, scores, NEG)
                new_peak = jnp.maximum(peak, jnp.max(scores, axis=0, keepdims=True))
                probs = jnp.exp(scores - new_peak)
                decay = jnp.exp(peak - new_peak)
                total = total * decay + jnp.sum(probs, axis=0, keepdims=True)
                v_part = vt_all[pl.ds(head * HD, HD), place]
                mixed = mixed * decay + mm(v_part, probs.astype(jnp.bfloat16))
                out.append((new_peak, total, mixed))
            return tuple(out)

        state = tuple(
            (
                jnp.full((1, BLK), NEG, jnp.float32),
                jnp.zeros((1, BLK), jnp.float32),
                jnp.zeros((HD, BLK), jnp.float32),
            )
            for _ in range(heads)
        )
        state = lax.fori_loop(mid, query_block, functools.partial(one_key, False), state)
        state = lax.fori_loop(low, mid + 1, functools.partial(one_key, True), state)
        both = jnp.concatenate([mixed / total for _, total, mixed in state], axis=0)
        o_all[here, :] = both.T.astype(jnp.bfloat16)
        for head in range(heads):
            peak, total, _ = state[head]
            l_all[pl.ds(head, 1), here] = peak + jnp.log(total)
        return carry

    lax.fori_loop(0, group * per_own, one_query, 0)
    for at in range(group):
        span = slice(at * own, (at + 1) * own)
        o_refs[at][...] = o_all[span, :]
        for head in range(heads):
            l_refs[at][head // 2, pl.ds(head % 2, 1), :] = l_all[pl.ds(head, 1), span]


def attend_forward(info, queries, keys_rot, values, chunks, after=()):
    own, width = queries[0].shape
    count, group = len(keys_rot), len(chunks)
    rows, pairs = own * count, width // PAIR
    together = 1
    wide_pair = together * PAIR
    steps = own * group * rows // 2
    column = pl.BlockSpec((own, wide_pair), lambda p, s: (0, p))
    outs = pl.pallas_call(
        functools.partial(attend_forward_kernel, tuple(chunks), count, own // BLK, len(after)),
        grid_spec=pltpu.PrefetchScalarGridSpec(
            num_scalar_prefetch=1,
            grid=(pairs // together,),
            in_specs=[pl.BlockSpec(memory_space=pl.ANY)] * len(after) + [column] * (group + 2 * count),
            out_specs=[column] * group
            + [pl.BlockSpec((together, 2, own), lambda p, s: (p, 0, 0))] * group,
            scratch_shapes=[
                pltpu.VMEM((group * own, wide_pair), jnp.bfloat16),
                pltpu.VMEM((group * own, wide_pair), jnp.bfloat16),
                pltpu.VMEM((max(2 * together, 8), group * own), jnp.float32),
                pltpu.VMEM((rows, wide_pair), jnp.bfloat16),
                pltpu.VMEM((wide_pair, rows), jnp.bfloat16),
            ],
        ),
        out_shape=[jax.ShapeDtypeStruct((own, width), jnp.bfloat16)] * group
        + [jax.ShapeDtypeStruct((pairs, 2, own), jnp.float32)] * group,
        compiler_params=pltpu.CompilerParams(vmem_limit_bytes=VMEM_LIMIT),
        cost_estimate=spend(
            flops=THRIFT * 16 * steps * width, bytes_accessed=8 * rows * width, transcendentals=steps * width // HD
        ),
        name="attend_forward",
    )(info, *after, *[queries[chunk] for chunk in chunks], *keys_rot, *values)
    return (outs[:group], outs[group:])


def spin(values, cosines, sines_low, sines_high, sign):
    ahead = pltpu.roll(values, PAIR - ROT // 2, 1)
    behind = pltpu.roll(values, ROT // 2, 1)
    return values * cosines + sign * (ahead * sines_low + behind * sines_high)


def attend_backward_kernel(count, pieces, per_own, after, info_ref, *refs):
    do_refs, refs = refs[after : after + pieces], refs[after + pieces :]
    q_refs, k_refs, v_refs, o_refs, l_refs = [
        refs[at * count : (at + 1) * count] for at in range(5)
    ]
    c_ref, sl_ref, sh_ref, out_ref, sum_ref, *scratch = refs[5 * count :]
    q_all, do_all, o_all, l_all, k_all, kt_all, v_all, dk_sum, dv_sum = scratch
    tensor_at = info_ref[2]
    own = per_own * BLK
    heads = k_all.shape[1] // HD
    spans = [slice(head // 2 * PAIR, head // 2 * PAIR + PAIR) for head in range(heads)]
    for at in range(count):
        span = slice(at * own, (at + 1) * own)
        k_all[span, :] = k_refs[at][...]
        kt_all[:, span] = k_refs[at][...].T
        v_all[span, :] = v_refs[at][...]
        q_all[span, :] = q_refs[at][...]
        o_all[span, :] = o_refs[at][...]
        for head in range(heads):
            l_all[pl.ds(head, 1), span] = l_refs[at][head // 2, pl.ds(head % 2, 1), :]
    done = 0
    for one in do_refs:
        do_all[done : done + one.shape[0], :] = one[...]
        done += one.shape[0]
    dk_sum[...] = jnp.zeros_like(dk_sum)
    dv_sum[...] = jnp.zeros_like(dv_sum)
    masks = lane_masks()

    def one_query(local_block, carry):
        query_block = swap_block(local_block, tensor_at, per_own)
        here = aligned(local_block)
        q_block = q_all[here, :]
        do_block = do_all[here, :]
        q_heads = [
            q_block[:, spans[head]] * (masks[head % 2] * HD ** (-0.5)).astype(jnp.bfloat16)
            for head in range(heads)
        ]
        do_heads = [do_block[:, spans[head]] * masks[head % 2] for head in range(heads)]
        prod = (do_block.astype(jnp.float32) * o_all[here, :].astype(jnp.float32)).T
        deltas = [
            jnp.sum(prod[head * HD : (head + 1) * HD], axis=0, keepdims=True) for head in range(heads)
        ]
        logs = [l_all[pl.ds(head, 1), here] for head in range(heads)]
        low, mid = key_range(info_ref, query_block)

        def one_key(masked, step, state):
            key_block = jnp.where(step < mid, step, query_block) if masked else step
            place = aligned(swap_block(key_block, tensor_at, per_own))
            k_block = k_all[place, :]
            v_block = v_all[place, :]
            if masked:
                allowed = allowed_block(info_ref, key_block, query_block)
            out, dk_parts, dv_parts = [], [], []
            for head in range(heads):
                probs = jnp.exp(mm(k_block[:, spans[head]], q_heads[head], NT) - logs[head])
                if masked:
                    probs = jnp.where(allowed, probs, 0.0)
                dprobs = mm(v_block[:, spans[head]], do_heads[head], NT)
                dscores = (probs * (dprobs - deltas[head])).astype(jnp.bfloat16)
                dv_parts.append(mm(probs.astype(jnp.bfloat16), do_heads[head]))
                dk_parts.append(mm(dscores, q_heads[head]))
                out.append(state[head] + mm(kt_all[pl.ds(head * HD, HD), place], dscores))
            for head in range(0, heads, 2):
                dk_sum[place, spans[head]] += dk_parts[head] + dk_parts[head + 1]
                dv_sum[place, spans[head]] += dv_parts[head] + dv_parts[head + 1]
            return tuple(out)

        state = tuple(jnp.zeros((HD, BLK), jnp.float32) for _ in range(heads))
        state = lax.fori_loop(mid, query_block, functools.partial(one_key, False), state)
        state = lax.fori_loop(low, mid + 1, functools.partial(one_key, True), state)
        dq = jnp.concatenate(state, axis=0).T * HD ** (-0.5)
        for span in spans[::2]:
            out_ref[0, here, span] = spin(
                dq[:, span], c_ref[here, :], sl_ref[here, :], sh_ref[here, :], -1.0
            ).astype(jnp.bfloat16)
        return carry

    lax.fori_loop(0, count * per_own, one_query, 0)
    for span in spans[::2]:
        out_ref[1, :, span] = spin(
            dk_sum[:, span], c_ref[...], sl_ref[...], sh_ref[...], -1.0
        ).astype(jnp.bfloat16)
    out_ref[2] = dv_sum[...].astype(jnp.bfloat16)
    for part in range(3):
        sum_ref[pl.ds(part, 1), :] = jnp.sum(
            out_ref[part].astype(jnp.float32), axis=0, keepdims=True
        )


def attend_backward(
    info, queries, keys_rot, values, grad_mix, mixed, logs, tables, first, pairs, held=(), after=()
):
    own, full = queries[0].shape
    count = len(queries)
    rows, width = own * count, pairs * PAIR
    together = 1
    shift = first // together
    steps = rows * rows // 2
    column = pl.BlockSpec((own, together * PAIR), lambda p, s: (0, p + shift))
    line = pl.BlockSpec((together, 2, own), lambda p, s: (p + shift, 0, 0))
    table = pl.BlockSpec((rows, PAIR), lambda p, s: (0, 0))
    far = list(held) + list(after)
    return pl.pallas_call(
        functools.partial(
            attend_backward_kernel, count, len(grad_mix), own // BLK, len(far)
        ),
        grid_spec=pltpu.PrefetchScalarGridSpec(
            num_scalar_prefetch=1,
            grid=(pairs // together,),
            in_specs=[pl.BlockSpec(memory_space=pl.ANY)] * len(far)
            + [
                pl.BlockSpec((one.shape[0], together * PAIR), lambda p, s: (0, p + shift))
                for one in grad_mix
            ]
            + [column] * (4 * count)
            + [line] * count
            + [table] * 3,
            out_specs=[
                pl.BlockSpec((3, rows, together * PAIR), lambda p, s: (0, 0, p + shift)),
                pl.BlockSpec((3, together * PAIR), lambda p, s: (0, p)),
            ],
            scratch_shapes=[
                pltpu.VMEM((rows, together * PAIR), jnp.bfloat16),
                pltpu.VMEM((rows, together * PAIR), jnp.bfloat16),
                pltpu.VMEM((rows, together * PAIR), jnp.bfloat16),
                pltpu.VMEM((max(2 * together, 8), rows), jnp.float32),
                pltpu.VMEM((rows, together * PAIR), jnp.bfloat16),
                pltpu.VMEM((together * PAIR, rows), jnp.bfloat16),
                pltpu.VMEM((rows, together * PAIR), jnp.bfloat16),
                pltpu.VMEM((rows, together * PAIR), jnp.float32),
                pltpu.VMEM((rows, together * PAIR), jnp.float32),
            ],
        ),
        out_shape=[
            jax.ShapeDtypeStruct((3, rows, full), jnp.bfloat16),
            jax.ShapeDtypeStruct((3, width), jnp.float32),
        ],
        input_output_aliases={1: 0} if held else {},
        compiler_params=pltpu.CompilerParams(vmem_limit_bytes=VMEM_LIMIT),
        cost_estimate=spend(
            flops=THRIFT * 40 * steps * width, bytes_accessed=16 * rows * width, transcendentals=steps * width // HD
        ),
        name="attend_backward",
    )(info, *far, *grad_mix, *queries, *keys_rot, *values, *mixed, *logs, *tables)


def project_kernel(x_ref, w_ref, b_ref, c_ref, sl_ref, sh_ref, q_ref, k_ref, v_ref):
    rows_in = x_ref[...]
    width = q_ref.shape[1]
    for part, out_ref in enumerate((q_ref, k_ref, v_ref)):
        full = mm(rows_in, w_ref[part]) + b_ref[pl.ds(part, 1), :]
        if part == 2:
            out_ref[...] = full.astype(jnp.bfloat16)
            continue
        for at in range(0, width, PAIR):
            piece = full[:, at : at + PAIR]
            out_ref[:, at : at + PAIR] = spin(
                piece, c_ref[...], sl_ref[...], sh_ref[...], 1.0
            ).astype(jnp.bfloat16)


def project(normed, weight, bias, tables, chunk=0):
    rows, depth = normed.shape
    width = weight.shape[2]
    block = min(rows, 256)
    first = chunk * rows // block
    table = pl.BlockSpec((block, PAIR), lambda i: (i + first, 0))
    return pl.pallas_call(
        project_kernel,
        grid=(rows // block,),
        in_specs=[
            pl.BlockSpec((block, depth), lambda i: (i, 0)),
            pl.BlockSpec((3, depth, width), lambda i: (0, 0, 0)),
            pl.BlockSpec((3, width), lambda i: (0, 0)),
            table,
            table,
            table,
        ],
        out_specs=[pl.BlockSpec((block, width), lambda i: (i, 0))] * 3,
        out_shape=[jax.ShapeDtypeStruct((rows, width), jnp.bfloat16)] * 3,
        compiler_params=pltpu.CompilerParams(vmem_limit_bytes=VMEM_LIMIT),
        cost_estimate=spend(
            flops=6 * rows * depth * width, bytes_accessed=2 * rows * depth + 6 * (rows + depth) * width, transcendentals=0
        ),
        name="project",
    )(normed, weight, bias, *tables)


def copy_in(source, target, sem):
    made = pltpu.make_async_copy(source, target, sem)
    made.start()
    return made


def feed_kernel(held, split, cut, after, *refs):
    refs = refs[after:]
    x_hbm, dy_hbm, refs = refs[:split], refs[split : split + cut], refs[split + cut :]
    gu_hbm, wd_hbm = refs[:2]
    z_ref, dgu_ref, da_ref = refs[2 + held : 5 + held]
    x_in, dy_in, wg_in, wu_in, wd_in, gate, up, inner_all, sems = refs[5 + held :]
    depth = x_in.shape[1]
    half = depth // 2
    rows = x_in.shape[0]
    piece, slab = rows // split, rows // cut
    get_x = [
        copy_in(x_hbm[at], x_in.at[pl.ds(at * piece, piece)], sems.at[5 + at]) for at in range(split)
    ]
    get_g0 = copy_in(gu_hbm.at[0, pl.ds(0, half)], wg_in.at[pl.ds(0, half)], sems.at[1])
    get_g1 = copy_in(gu_hbm.at[0, pl.ds(half, half)], wg_in.at[pl.ds(half, half)], sems.at[2])
    for one in get_x:
        one.wait()
    get_g0.wait()
    get_u = copy_in(gu_hbm.at[1], wu_in, sems.at[3])
    gate[...] = mm(x_in[:, :half], wg_in[:half])
    get_g1.wait()
    get_dy = [
        copy_in(dy_hbm[at], dy_in.at[pl.ds(at * slab, slab)], sems.at[7 + at])
        for at in range(cut)
    ]
    get_d = copy_in(wd_hbm, wd_in, sems.at[4])
    gate[...] += mm(x_in[:, half:], wg_in[half:])
    get_u.wait()
    up[...] = mm(x_in[...], wu_in[...])
    for one in get_dy:
        one.wait()
    get_d.wait()
    hidden = wd_in.shape[0]
    for at in range(0, hidden, BLK):
        span = slice(at, min(at + BLK, hidden))
        inner_all[:, span] = mm(dy_in[...], wd_in[span, :], NT)
    step = 64

    def middle(at, carry):
        here = pl.ds(pl.multiple_of(at * step, step), step)
        gate_pre, up_pre, inner = gate[here, :], up[here, :], inner_all[here, :]
        sigmoid_gate = 1.0 / (1.0 + jnp.exp(-gate_pre))
        activated = gate_pre * sigmoid_gate
        z_ref[here, :] = (activated * up_pre).astype(jnp.bfloat16)
        dgu_ref[0, here, :] = (
            inner * up_pre * (sigmoid_gate * (1.0 + gate_pre * (1.0 - sigmoid_gate)))
        ).astype(jnp.bfloat16)
        dgu_ref[1, here, :] = (inner * activated).astype(jnp.bfloat16)
        return carry

    lax.fori_loop(0, rows // step, middle, 0)

    def back(at, carry):
        here = pl.ds(pl.multiple_of(at * BLK, BLK), BLK)
        da_ref[:, here] = (
            mm(dgu_ref[0], wg_in[here, :], NT) + mm(dgu_ref[1], wu_in[here, :], NT)
        ).astype(da_ref.dtype)
        return carry

    lax.fori_loop(0, depth // BLK, back, 0)


def feed(chunk, count, normed, back, gate_up, down, held, after=()):
    split, cut = len(normed), len(back)
    rows, depth = normed[0].shape[0] * split, normed[0].shape[1]
    hidden = down.shape[0]
    far = pl.BlockSpec(memory_space=pl.ANY)
    return pl.pallas_call(
        functools.partial(feed_kernel, len(held), split, cut, len(after)),
        grid=(1,),
        in_specs=[far] * (2 + split + cut + len(held) + len(after)),
        out_specs=[
            pl.BlockSpec((rows, hidden), lambda i: (chunk, 0)),
            pl.BlockSpec((2, rows, hidden), lambda i: (0, chunk, 0)),
            pl.BlockSpec((rows, depth), lambda i: (0, 0)),
        ],
        out_shape=[
            jax.ShapeDtypeStruct((rows * count, hidden), jnp.bfloat16),
            jax.ShapeDtypeStruct((2, rows * count, hidden), jnp.bfloat16),
            jax.ShapeDtypeStruct((rows, depth), jnp.float32 if chunk == 0 else jnp.bfloat16),
        ],
        input_output_aliases={len(after) + 2 + split + cut + at: at for at in range(len(held))},
        scratch_shapes=[
            pltpu.VMEM((rows, depth), jnp.bfloat16),
            pltpu.VMEM((rows, depth), jnp.bfloat16),
            pltpu.VMEM((depth, hidden), jnp.bfloat16),
            pltpu.VMEM((depth, hidden), jnp.bfloat16),
            pltpu.VMEM((hidden, depth), jnp.bfloat16),
            pltpu.VMEM((rows, hidden), jnp.float32),
            pltpu.VMEM((rows, hidden), jnp.float32),
            pltpu.VMEM((rows, hidden), jnp.float32),
            pltpu.SemaphoreType.DMA((9,)),
        ],
        compiler_params=pltpu.CompilerParams(vmem_limit_bytes=VMEM_LIMIT),
        cost_estimate=spend(
            flops=10 * rows * depth * hidden, bytes_accessed=6 * depth * hidden, transcendentals=rows * hidden
        ),
        name="feed",
    )(*after, *normed, *back, gate_up, down, *held)


def wide_grad_kernel(count, after, *refs):
    refs = refs[after:]
    lefts, (right, out, turned) = refs[:count], refs[count:]
    done = 0
    for left in lefts:
        turned[:, done : done + left.shape[0]] = left[...].T
        done += left.shape[0]
    for part in range(out.shape[0]):
        out[part] = mm(turned[...], right[part]).astype(jnp.bfloat16)


def wide_grad(lefts, right, after=(), column=0, cuts=1):
    depth = lefts[0].shape[1]
    parts, rows, width = right.shape
    width = width // cuts
    return pl.pallas_call(
        functools.partial(wide_grad_kernel, len(lefts), len(after)),
        grid=(depth // BLK,),
        in_specs=[pl.BlockSpec(memory_space=pl.ANY)] * len(after)
        + [pl.BlockSpec((left.shape[0], BLK), lambda i: (0, i)) for left in lefts]
        + [pl.BlockSpec((parts, rows, width), lambda i: (0, 0, column))],
        out_specs=pl.BlockSpec((parts, BLK, width), lambda i: (0, i, 0)),
        out_shape=jax.ShapeDtypeStruct((parts, depth, width), jnp.bfloat16),
        scratch_shapes=[pltpu.VMEM((BLK, rows), jnp.bfloat16)],
        compiler_params=pltpu.CompilerParams(vmem_limit_bytes=VMEM_LIMIT),
        cost_estimate=spend(
            flops=2 * rows * depth * width * parts,
            bytes_accessed=2 * (rows * depth + parts * width * (rows + depth)),
            transcendentals=0,
        ),
        name="wide_grad",
    )(*after, *lefts, right)


def tall_grad_kernel(held, count, after, *refs):
    refs = refs[after:]
    lefts, rights, (out, turned, joined) = refs[:held], refs[held : held + count], refs[held + count :]
    tall = lefts[0].shape[0]

    @pl.when(pl.program_id(0) == 0)
    def _():
        for at in range(held):
            turned[:, at * tall : (at + 1) * tall] = lefts[at][...].T

    done = 0
    for right in rights:
        joined[done : done + right.shape[0], :] = right[...]
        done += right.shape[0]
    out[...] = mm(turned[...], joined[...]).astype(jnp.bfloat16)


def tall_grad(lefts, rights, after=()):
    tall, depth = lefts[0].shape
    width = rights[0].shape[1]
    count, held = len(rights), len(lefts)
    rows = tall * held
    return pl.pallas_call(
        functools.partial(tall_grad_kernel, held, count, len(after)),
        grid=(width // BLK,),
        in_specs=[pl.BlockSpec(memory_space=pl.ANY)] * len(after)
        + [pl.BlockSpec((tall, depth), lambda i: (0, 0))] * held
        + [pl.BlockSpec((right.shape[0], BLK), lambda i: (0, i)) for right in rights],
        out_specs=pl.BlockSpec((depth, BLK), lambda i: (0, i)),
        out_shape=jax.ShapeDtypeStruct((depth, width), jnp.bfloat16),
        scratch_shapes=[
            pltpu.VMEM((depth, rows), jnp.bfloat16),
            pltpu.VMEM((rows, BLK), jnp.bfloat16),
        ],
        compiler_params=pltpu.CompilerParams(vmem_limit_bytes=VMEM_LIMIT),
        cost_estimate=spend(
            flops=2 * rows * depth * width,
            bytes_accessed=2 * (rows * depth + width * (rows + depth)),
            transcendentals=0,
        ),
        name="tall_grad",
    )(*after, *lefts, *rights)


FAR = pl.BlockSpec(memory_space=pl.ANY)


def halves_kernel(after, count, *refs):
    for source, target in zip(refs[after : after + count], refs[after + count :]):
        target[...] = source[...]


def halves(picks, after=()):
    half, depth = picks[0][0].shape[0] // 2, picks[0][0].shape[1]
    specs = [
        pl.BlockSpec((half, depth), functools.partial(lambda which, i: (which, 0), which))
        for _, which in picks
    ]
    return pl.pallas_call(
        functools.partial(halves_kernel, len(after), len(picks)),
        grid=(1,),
        in_specs=[FAR] * len(after) + specs,
        out_specs=[pl.BlockSpec((half, depth), lambda i: (0, 0))] * len(picks),
        out_shape=[jax.ShapeDtypeStruct((half, depth), picks[0][0].dtype)] * len(picks),
        compiler_params=pltpu.CompilerParams(vmem_limit_bytes=VMEM_LIMIT),
        cost_estimate=spend(
            flops=half * depth, bytes_accessed=4 * len(picks) * half * depth, transcendentals=0
        ),
        name="halves",
    )(*after, *[one for one, _ in picks])


def join_kernel(after, *refs):
    top, end, out = refs[after:]
    half = top.shape[0]
    out[:half, :] = top[...]
    out[half:, :] = end[...]


def join(top, end, after=()):
    half, depth = top.shape
    whole = pl.BlockSpec((half, depth), lambda i: (0, 0))
    return pl.pallas_call(
        functools.partial(join_kernel, len(after)),
        grid=(1,),
        in_specs=[FAR] * len(after) + [whole, whole],
        out_specs=pl.BlockSpec((2 * half, depth), lambda i: (0, 0)),
        out_shape=jax.ShapeDtypeStruct((2 * half, depth), top.dtype),
        compiler_params=pltpu.CompilerParams(vmem_limit_bytes=VMEM_LIMIT),
        cost_estimate=spend(flops=half * depth, bytes_accessed=8 * half * depth, transcendentals=0),
        name="join",
    )(*after, top, end)


def shrink_kernel(after, *refs):
    source, scale, out = refs[after:]
    out[...] = (source[...].astype(jnp.float32) * scale[...]).astype(jnp.bfloat16)


def shrink(values, scale, after=()):
    rows, depth = values.shape
    block = rows // 4
    return pl.pallas_call(
        functools.partial(shrink_kernel, len(after)),
        grid=(4,),
        in_specs=[FAR] * len(after)
        + [
            pl.BlockSpec((block, depth), lambda i: (i, 0)),
            pl.BlockSpec((block, 1), lambda i: (i, 0)),
        ],
        out_specs=pl.BlockSpec((block, depth), lambda i: (i, 0)),
        out_shape=jax.ShapeDtypeStruct((rows, depth), jnp.bfloat16),
        compiler_params=pltpu.CompilerParams(vmem_limit_bytes=VMEM_LIMIT),
        cost_estimate=spend(
            flops=rows * depth, bytes_accessed=6 * rows * depth, transcendentals=0
        ),
        name="shrink",
    )(*after, values, scale)


LINES = 128


def arrived(own, parts, steps):
    total = own[...].astype(jnp.float32)
    if parts:
        first = pl.program_id(0) < steps // 2
        one, two, three, four = [part[...].astype(jnp.float32) for part in parts]
        total = total + jnp.where(first, one + two, three + four)
    return total


def part_specs(parts, depth, steps):
    if not parts:
        return []
    top = pl.BlockSpec((LINES, depth), lambda i: (jnp.minimum(i, steps // 2 - 1), 0))
    end = pl.BlockSpec((LINES, depth), lambda i: (jnp.maximum(i - steps // 2, 0), 0))
    return [top, top, end, end]


def unit_of(values):
    average = jnp.mean(values, axis=-1, keepdims=True)
    centered = values - average
    inverse = lax.rsqrt(jnp.mean(centered * centered, axis=-1, keepdims=True) + NORM_EPS)
    return (centered * inverse, inverse)


def settle_kernel(held, after, steps, *refs):
    refs = refs[after:]
    own, parts = refs[0], refs[1 : 1 + held]
    resid, gain, shift, hidden, normed = refs[1 + held :]
    values = resid[...].astype(jnp.float32) + arrived(own, parts, steps)
    hidden[...] = values
    normed[...] = (unit_of(values)[0] * gain[...] + shift[...]).astype(jnp.bfloat16)


def settle(own, parts, resid, gain, shift, after=()):
    rows, depth = own.shape
    steps = rows // LINES
    block = pl.BlockSpec((LINES, depth), lambda i: (i, 0))
    line = pl.BlockSpec((1, depth), lambda i: (0, 0))
    return pl.pallas_call(
        functools.partial(settle_kernel, len(parts), len(after), steps),
        grid=(steps,),
        in_specs=[FAR] * len(after)
        + [block]
        + part_specs(parts, depth, steps)
        + [block, line, line],
        out_specs=[block, block],
        out_shape=[
            jax.ShapeDtypeStruct((rows, depth), jnp.float32),
            jax.ShapeDtypeStruct((rows, depth), jnp.bfloat16),
        ],
        compiler_params=pltpu.CompilerParams(vmem_limit_bytes=VMEM_LIMIT),
        cost_estimate=spend(
            flops=10 * rows * depth, bytes_accessed=16 * rows * depth, transcendentals=rows
        ),
        name="settle",
    )(*after, own, *parts, resid, gain, shift)


def finish_kernel(held, after, steps, *refs):
    refs = refs[after:]
    own, parts = refs[0], refs[1 : 1 + held]
    hidden, out = refs[1 + held :]
    total = hidden[...] + arrived(own, parts, steps)
    out[...] = total.astype(jnp.bfloat16)


def finish(own, parts, hidden, after=()):
    rows, depth = own.shape
    steps = rows // LINES
    block = pl.BlockSpec((LINES, depth), lambda i: (i, 0))
    return pl.pallas_call(
        functools.partial(finish_kernel, len(parts), len(after), steps),
        grid=(steps,),
        in_specs=[FAR] * len(after) + [block] + part_specs(parts, depth, steps) + [block],
        out_specs=block,
        out_shape=jax.ShapeDtypeStruct((rows, depth), jnp.bfloat16),
        compiler_params=pltpu.CompilerParams(vmem_limit_bytes=VMEM_LIMIT),
        cost_estimate=spend(
            flops=4 * rows * depth, bytes_accessed=12 * rows * depth, transcendentals=0
        ),
        name="finish",
    )(*after, own, *parts, hidden)


def unsettle_kernel(held, after, steps, *refs):
    refs = refs[after:]
    own, parts = refs[0], refs[1 : 1 + held]
    values, extra, gain, total, short, gain_sum, shift_sum = refs[1 + held :]
    incoming = arrived(own, parts, steps)
    unit_rows, inverse = unit_of(values[...].astype(jnp.float32))
    scaled = incoming * gain[...]
    grad_rows = inverse * (
        scaled
        - jnp.mean(scaled, axis=-1, keepdims=True)
        - unit_rows * jnp.mean(scaled * unit_rows, axis=-1, keepdims=True)
    )
    result = extra[...].astype(jnp.float32) + grad_rows
    total[...] = result
    short[...] = result.astype(jnp.bfloat16)

    @pl.when(pl.program_id(0) == 0)
    def _():
        gain_sum[...] = jnp.zeros_like(gain_sum)
        shift_sum[...] = jnp.zeros_like(shift_sum)

    gain_sum[...] += jnp.sum(incoming * unit_rows, axis=0, keepdims=True)
    shift_sum[...] += jnp.sum(incoming, axis=0, keepdims=True)


def unsettle(own, parts, values, extra, gain, after=()):
    rows, depth = own.shape
    steps = rows // LINES
    block = pl.BlockSpec((LINES, depth), lambda i: (i, 0))
    line = pl.BlockSpec((1, depth), lambda i: (0, 0))
    return pl.pallas_call(
        functools.partial(unsettle_kernel, len(parts), len(after), steps),
        grid=(steps,),
        in_specs=[FAR] * len(after)
        + [block]
        + part_specs(parts, depth, steps)
        + [block, block, line],
        out_specs=[block, block, line, line],
        out_shape=[
            jax.ShapeDtypeStruct((rows, depth), jnp.float32),
            jax.ShapeDtypeStruct((rows, depth), jnp.bfloat16),
            jax.ShapeDtypeStruct((1, depth), jnp.float32),
            jax.ShapeDtypeStruct((1, depth), jnp.float32),
        ],
        compiler_params=pltpu.CompilerParams(vmem_limit_bytes=VMEM_LIMIT),
        cost_estimate=spend(
            flops=20 * rows * depth, bytes_accessed=20 * rows * depth, transcendentals=rows
        ),
        name="unsettle",
    )(*after, own, *parts, values, extra, gain)


def unproject_kernel(count, after, *refs):
    refs = refs[after:]
    lefts, w_ref, outs = refs[:count], refs[count], refs[count + 1 :]
    own = outs[0].shape[0]
    total = None
    for part in range(3):
        left = jnp.concatenate([one[part] for one in lefts], axis=0)
        made = mm(left, w_ref[part], NT)
        total = made if total is None else total + made
    for at, out in enumerate(outs):
        out[...] = total[at * own : (at + 1) * own].astype(out.dtype)


def unproject(grads, weight, chunks, own, after=()):
    parts, depth, width = weight.shape
    count = len(chunks)
    return pl.pallas_call(
        functools.partial(unproject_kernel, count, len(after)),
        grid=(depth // BLK,),
        in_specs=[FAR] * len(after)
        + [
            pl.BlockSpec((parts, own, width), functools.partial(lambda which, i: (0, which, 0), chunk))
            for chunk in chunks
        ]
        + [pl.BlockSpec((parts, BLK, width), lambda i: (0, i, 0))],
        out_specs=[pl.BlockSpec((own, BLK), lambda i: (0, i))] * count,
        out_shape=[
            jax.ShapeDtypeStruct((own, depth), jnp.bfloat16 if chunk else jnp.float32)
            for chunk in chunks
        ],
        compiler_params=pltpu.CompilerParams(vmem_limit_bytes=VMEM_LIMIT),
        cost_estimate=spend(
            flops=2 * parts * own * count * depth * width,
            bytes_accessed=2 * parts * width * (own * count + depth) + 4 * own * count * depth,
            transcendentals=0,
        ),
        name="unproject",
    )(*after, *[grads] * count, weight)


def adam_kernel(rate, decay, after, *refs):
    weight, gradient, first, second, grad_out, first_out, second_out, weight_out = refs[after:]
    grad = gradient[...].astype(jnp.float32)
    grad_out[...] = grad
    first_out[...], second_out[...], weight_out[...] = adam_update(
        weight[...], grad, first[...], second[...], rate, decay
    )


def adam(weight, gradient, first, second, rate, after=()):
    shape = weight.shape
    flat = (-1, shape[-1])
    arrays = [one.reshape(flat) for one in (weight, gradient, first, second)]
    rows, width = arrays[0].shape
    block = pl.BlockSpec((rows // 4, width), lambda i: (i, 0))
    outs = pl.pallas_call(
        functools.partial(adam_kernel, rate, WEIGHT_DECAY, len(after)),
        grid=(4,),
        in_specs=[FAR] * len(after) + [block] * 4,
        out_specs=[block] * 4,
        out_shape=[jax.ShapeDtypeStruct((rows, width), jnp.float32)] * 4,
        compiler_params=pltpu.CompilerParams(vmem_limit_bytes=VMEM_LIMIT),
        cost_estimate=spend(
            flops=12 * rows * width, bytes_accessed=30 * rows * width, transcendentals=0
        ),
        name="adam",
    )(*after, *arrays)
    return [one.reshape(shape) for one in outs]


def hold(values, after):
    rows, depth = values.shape
    whole = pl.BlockSpec((rows, depth), lambda i: (0, 0))

    def body(*refs):
        refs[-1][...] = refs[-2][...]

    return pl.pallas_call(
        body,
        grid=(1,),
        in_specs=[FAR] * len(after) + [whole],
        out_specs=whole,
        out_shape=jax.ShapeDtypeStruct((rows, depth), values.dtype),
        cost_estimate=spend(
            flops=rows * depth, bytes_accessed=8 * rows * depth, transcendentals=0
        ),
        name="hold",
    )(*after, values)


def first_line_kernel(after, *refs):
    w_ref, first_ref, second_ref, sum_ref, out_ref = refs[after:]
    cut = first_ref.shape[2]
    gain, shift = None, None
    for part in range(3):
        weight = w_ref[part].astype(jnp.float32)
        grad = jnp.concatenate([first_ref[part], second_ref[part]], axis=1).astype(jnp.float32)
        gain = weight * grad if gain is None else gain + weight * grad
        lean = weight * sum_ref[pl.ds(part, 1), :]
        shift = lean if shift is None else shift + lean
    out_ref[pl.ds(0, 1), :] = jnp.sum(gain.T, axis=0, keepdims=True)
    out_ref[pl.ds(1, 1), :] = jnp.sum(shift.T, axis=0, keepdims=True)


def first_line(weight, first, second, sums, after):
    parts, depth, width = weight.shape
    cut = first.shape[2]
    return pl.pallas_call(
        functools.partial(first_line_kernel, len(after)),
        grid=(depth // BLK,),
        in_specs=[FAR] * len(after)
        + [
            pl.BlockSpec((parts, BLK, width), lambda i: (0, i, 0)),
            pl.BlockSpec((parts, BLK, cut), lambda i: (0, i, 0)),
            pl.BlockSpec((parts, BLK, width - cut), lambda i: (0, i, 0)),
            pl.BlockSpec((parts, width), lambda i: (0, 0)),
        ],
        out_specs=pl.BlockSpec((2, BLK), lambda i: (0, i)),
        out_shape=jax.ShapeDtypeStruct((2, depth), jnp.float32),
        compiler_params=pltpu.CompilerParams(vmem_limit_bytes=VMEM_LIMIT),
        cost_estimate=spend(
            flops=4 * parts * depth * width, bytes_accessed=4 * parts * depth * width, transcendentals=0
        ),
        name="first_line",
    )(*after, weight, first, second, sums)


def down_project_kernel(after, count, *refs):
    z_ref, w_ref, outs = refs[after], refs[after + 1], refs[after + 2 :]
    for at in range(count):

        @pl.when(pl.program_id(0) == at)
        def _():
            outs[at][...] = mm(z_ref[...], w_ref[...]).astype(jnp.bfloat16)


def down_project(inner, weight, count, after=()):
    rows, hidden = inner.shape
    depth = weight.shape[1]
    own = rows // count
    return pl.pallas_call(
        functools.partial(down_project_kernel, len(after), count),
        grid=(count,),
        in_specs=[FAR] * len(after)
        + [
            pl.BlockSpec((own, hidden), lambda i: (i, 0)),
            pl.BlockSpec((hidden, depth), lambda i: (0, 0)),
        ],
        out_specs=[pl.BlockSpec((own, depth), lambda i: (0, 0))] * count,
        out_shape=[jax.ShapeDtypeStruct((own, depth), jnp.bfloat16)] * count,
        compiler_params=pltpu.CompilerParams(vmem_limit_bytes=VMEM_LIMIT),
        cost_estimate=spend(
            flops=2 * rows * depth * hidden,
            bytes_accessed=2 * (rows * depth + hidden * (rows + depth)),
            transcendentals=0,
        ),
        name="down_project",
    )(*after, inner, weight)


def lane_tables(position):
    half_rot = ROT // 2
    lane = jnp.arange(PAIR, dtype=jnp.int32) % HD
    freqs = 10000.0 ** (-((lane % half_rot).astype(jnp.float32) * (2.0 / ROT)))
    angles = position.astype(jnp.float32)[:, None] * freqs[None, :]
    cosines, sines = jnp.cos(angles), jnp.sin(angles)
    in_low, in_high = (lane < half_rot)[None], ((lane >= half_rot) & (lane < ROT))[None]
    return (
        jnp.where((lane < ROT)[None], cosines, 1.0),
        jnp.where(in_low, -sines, 0.0),
        jnp.where(in_high, sines, 0.0),
    )


def sequence_facts(lengths, owners, dp_index):
    owned = owners == dp_index
    total = jnp.sum(jnp.where(owned, lengths, 0))
    return (lengths[jnp.argmax(owned)], total)


def norm_forward(values, gain, shift):
    return unit_of(values)[0] * gain + shift


def adam_update(weight_old, gradient, first_old, second_old, rate, decay):
    first_new = BETA_ONE * first_old + (1.0 - BETA_ONE) * gradient
    second_new = BETA_TWO * second_old + (1.0 - BETA_TWO) * gradient * gradient
    first_hat = first_new / (1.0 - BETA_ONE**STEP)
    second_hat = second_new / (1.0 - BETA_TWO**STEP)
    weight_new = weight_old * (1.0 - rate * decay) - rate * first_hat / (
        jnp.sqrt(second_hat) + ADAM_EPS
    )
    return (first_new, second_new, weight_new)


def low(values):
    return values.astype(jnp.bfloat16)


def wide(values):
    return values.astype(jnp.float32)


def swap(values, axis, bits):
    size = lax.axis_size(axis)
    return lax.ppermute(values, axis, [(at, at ^ bits) for at in range(size)])


def gather_start(rows):
    count = lax.axis_size("tensor")
    if count != 4:
        return [swap(rows, "tensor", bits) for bits in range(1, count)]
    return [swap(rows, "tensor", 1), swap(rows, "tensor", 2)]


def gather_on(near, after=(), with_sends=False):
    passed, sends = (), ()
    if lax.axis_size("tensor") == 4:
        sends = halves([(near[0], 0), (near[1], 1)], after)
        passed = (swap(sends[0], "tensor", 2), swap(sends[1], "tensor", 1))
    return (passed, sends) if with_sends else passed


def pieces_of(pieces, chunk):
    return pieces[3:] if len(pieces) == 5 and chunk == 3 else [pieces[chunk]]


def scatter_start(parts, after=()):
    if lax.axis_size("tensor") != 4:
        return [swap(low(parts[bits]), "tensor", bits) for bits in range(1, len(parts))]
    _, one, two, three = parts
    half = one.shape[0] // 2
    if after:
        three_top, three_end, one_top, two_end = after
    else:
        three = low(three)
        three_top, three_end = three[:half], three[half:]
        one_top, two_end = low(one[:half]), low(two[half:])
    return [
        swap(three_top, "tensor", 1),
        swap(three_end, "tensor", 2),
        swap(one_top, "tensor", 1),
        swap(two_end, "tensor", 2),
    ]


def scatter_on(parts, moved):
    if lax.axis_size("tensor") != 4:
        return []
    _, one, two, _ = parts
    half = one.shape[0] // 2
    return [low(wide(one[half:]) + wide(moved[1])), low(wide(two[:half]) + wide(moved[0]))]


def scatter_end(parts, moved, passing=None):
    if lax.axis_size("tensor") != 4:
        total = wide(parts[0])
        for one in moved:
            total = total + wide(one)
        return (total, [])
    one_end, two_top = passing or scatter_on(parts, moved)
    return (
        parts[0],
        [moved[2], swap(two_top, "tensor", 2), swap(one_end, "tensor", 1), moved[3]],
    )


def sum_along(values, axis):
    bits = 1
    while bits < lax.axis_size(axis):
        values = values + swap(values, axis, bits)
        bits *= 2
    return values


def scatter_weight(partial):
    return lax.psum_scatter(partial, "dp", scatter_dimension=1, tiled=True)


def dot(left, right, dims):
    return lax.dot_general(left, right, (dims, ((), ())), preferred_element_type=jnp.float32)


def local(
    hidden_in,
    grad_out,
    lengths,
    owners,
    qkv_weight,
    out_weight,
    gate_up_weight,
    down_weight,
    norm_gain,
    norm_bias,
    qkv_bias,
    qkv_first,
    out_first,
    gate_up_first,
    down_first,
    small_first,
    qkv_second,
    out_second,
    gate_up_second,
    down_second,
    small_second,
):
    dp_index = lax.axis_index("dp")
    tp_index = lax.axis_index("tensor")
    count = lax.axis_size("tensor")
    own_rows = hidden_in.shape[0]
    local_width = qkv_weight.shape[2]
    chunks = list(range(count))
    groups = [[3], [1, 2], [0]] if count == 4 else [chunks[1:], [0]]
    qkv_full, out_full, gate_up_full, down_full = [
        lax.all_gather(low(one), "dp", axis=1, tiled=True)
        for one in (qkv_weight, out_weight, gate_up_weight, down_weight)
    ]
    split, total = sequence_facts(lengths, owners, dp_index)
    row_ids = jnp.concatenate(
        [(tp_index ^ chunk) * own_rows + jnp.arange(own_rows, dtype=jnp.int32) for chunk in chunks]
    )
    starts = jnp.where(row_ids < split, 0, jnp.where(row_ids < total, split, total))
    live_own = wide(row_ids[:own_rows] < total)
    info = jnp.stack([split, total, tp_index, tp_index]).astype(jnp.int32)
    lanes = lane_tables(row_ids - starts)
    bias_local = lax.dynamic_slice_in_dim(qkv_bias, tp_index * local_width, local_width, 1)

    first_norm = low(norm_forward(wide(hidden_in), norm_gain[0], norm_bias[0]))
    near = gather_start(first_norm)
    passed = gather_on(near)
    early = [
        project(one, qkv_full, bias_local, lanes, chunk)
        for chunk, one in enumerate([first_norm] + near)
    ]
    normed_one = [first_norm] + near
    if passed:
        normed_one.append(join(*passed, [one[0] for one in early]))
    projected = early + [
        project(normed_one[chunk], qkv_full, bias_local, lanes, chunk)
        for chunk in chunks[len(early) :]
    ]
    queries, keys_rot, values = [[one[part] for one in projected] for part in range(3)]
    cotangent = shrink(grad_out, live_own[:, None], normed_one[1:])
    near = gather_start(cotangent)
    passed = gather_on(near)
    back_ffn = [cotangent, *near] + ([join(*passed)] if passed else [])

    attn_mix, log_total = [None] * count, [None] * count
    for step, group in enumerate(groups):
        after = near if step == 1 else ()
        mixed, logs = attend_forward(info, queries, keys_rot, values, group, after)
        for at, chunk in enumerate(group):
            attn_mix[chunk], log_total[chunk] = mixed[at], logs[at]
    parts = [dot(one, out_full, ((1,), (0,))) for one in attn_mix]
    hidden, second_norm = settle(
        *scatter_end(parts, scatter_start(parts)),
        hidden_in,
        norm_gain[1:2],
        norm_bias[1:2],
    )

    near = gather_start(second_norm)
    held, back_second = (), [None] * count

    def feed_one(chunk, normed, held, after=()):
        *held, back_second[chunk] = feed(
            chunk, count, normed, pieces_of(back_ffn, chunk), gate_up_full, down_full, held, after
        )
        return held

    held = feed_one(0, [second_norm], held)
    passed = gather_on(near, held[:1])
    held = feed_one(1, near[:1], held)
    normed_two = [second_norm, *near, *passed]
    for chunk in [3, 2] if count == 4 else chunks[2:]:
        held = feed_one(chunk, pieces_of(normed_two, chunk), held)
    inner_act, grad_gate_up = held
    moved = scatter_start(back_second)
    passing = scatter_on(back_second, moved)
    gate_up_partial = wide_grad(normed_two, grad_gate_up, moved[:2] + passing)
    gate_up_grad = scatter_weight(gate_up_partial)
    layer_parts = down_project(inner_act, down_full, count, [gate_up_partial])
    grad_hidden, grad_hidden_low, gain_two_grad, bias_two_grad = unsettle(
        *scatter_end(back_second, moved, passing),
        hidden,
        cotangent,
        norm_gain[1:2],
        [gate_up_partial, *layer_parts],
    )
    near = gather_start(grad_hidden_low)
    down_partial = tall_grad([inner_act], back_ffn, [grad_hidden_low])
    down_grad = scatter_weight(down_partial)
    passed = gather_on(near, [down_partial])
    back_attn = [grad_hidden_low, *near, *passed]

    grad_mix = [low(dot(one, out_full, ((1,), (1,)))) for one in back_attn]
    layer_sends = []
    if count == 4:
        layer_sends = halves(
            [(layer_parts[3], 0), (layer_parts[3], 1), (layer_parts[1], 0), (layer_parts[2], 1)],
            back_attn[1:],
        )
    layer_moved = scatter_start(layer_parts, layer_sends)
    pairs = local_width // PAIR
    cut = pairs // 2
    saved = (info, queries, keys_rot, values, grad_mix, attn_mix, log_total, lanes)
    first_proj, first_sums = attend_backward(*saved, 0, cut, (), [gate_up_grad] + layer_moved[:2])
    first_partial = wide_grad(normed_one, first_proj, (), 0, 2)
    first_grad = scatter_weight(first_partial)
    out_partial = tall_grad(attn_mix, back_attn, [first_partial])
    out_grad = scatter_weight(out_partial)
    passing = scatter_on(layer_parts, layer_moved)
    grad_proj, second_sums = attend_backward(
        *saved, cut, pairs - cut, [first_proj], [out_partial] + passing
    )
    layer_own, layer_rest = scatter_end(layer_parts, layer_moved, passing)
    second_partial = wide_grad(
        normed_one, grad_proj, [first_grad] + layer_rest, 1, 2
    )
    parts = unproject(grad_proj, qkv_full, chunks, own_rows, [second_partial])
    moved = scatter_start(parts)
    onward = scatter_on(parts, moved)
    settled = scatter_end(parts, moved, onward)
    layer_out = finish(layer_own, layer_rest, hidden, parts[1:])
    second_grad = scatter_weight(second_partial)
    qkv_grad = wide(jnp.concatenate([first_grad, second_grad], axis=2))
    gate_up_grad = wide(gate_up_grad)
    input_grad = unsettle(
        *settled, hidden_in, grad_hidden, norm_gain[:1]
    )[0]

    bias_local_grad = jnp.concatenate([first_sums, second_sums], axis=1)
    lines = first_line(qkv_full, first_partial, second_partial, bias_local_grad, parts[1:])
    gain_one_grad = (lines[:1] - norm_bias[:1] * lines[1:]) / norm_gain[:1]
    bias_grad_full = lax.dynamic_update_slice_in_dim(
        jnp.zeros((3, qkv_bias.shape[1]), jnp.float32), bias_local_grad, tp_index * local_width, 1
    )
    small_grad = jnp.concatenate(
        [gain_one_grad, gain_two_grad, lines[1:], bias_two_grad, bias_grad_full], axis=0
    )
    small_weight = jnp.concatenate([norm_gain, norm_bias, qkv_bias], axis=0)
    qkv_first_new, qkv_second_new, qkv_new = adam_update(
        qkv_weight, qkv_grad, qkv_first, qkv_second, RATE_QKV, WEIGHT_DECAY
    )
    gate_up_first_new, gate_up_second_new, gate_up_new = adam_update(
        gate_up_weight, gate_up_grad, gate_up_first, gate_up_second, RATE_GATE_UP, WEIGHT_DECAY
    )
    settled_all = list(settled[1]) + [layer_out, gate_up_new]
    down_grad, down_first_new, down_second_new, down_new = adam(
        down_weight, down_grad, down_first, down_second, RATE_DOWN, settled[1]
    )
    out_grad, out_first_new, out_second_new, out_new = adam(
        out_weight, out_grad, out_first, out_second, RATE_OUT, settled[1]
    )
    small_grad = sum_along(sum_along(hold(small_grad, settled_all), "tensor"), "dp")
    small_first_new, small_second_new, small_new = adam_update(
        small_weight, small_grad, small_first, small_second, RATE_SMALL, 0.0
    )
    return (
        layer_out,
        input_grad,
        qkv_grad,
        qkv_first_new,
        qkv_second_new,
        qkv_new,
        out_grad,
        out_first_new,
        out_second_new,
        out_new,
        gate_up_grad,
        gate_up_first_new,
        gate_up_second_new,
        gate_up_new,
        down_grad,
        down_first_new,
        down_second_new,
        down_new,
        small_grad,
        small_first_new,
        small_second_new,
        small_new,
    )


def solution(mesh):
    placed = (
        P(("dp", "tensor"), None),
        P(("dp", "tensor"), None),
        P(),
        P(),
        P(None, "dp", "tensor"),
        P("tensor", "dp"),
        P(None, "dp", "tensor"),
        P("tensor", "dp"),
        P(),
        P(),
        P(),
        P(None, "dp", "tensor"),
        P("tensor", "dp"),
        P(None, "dp", "tensor"),
        P("tensor", "dp"),
        P(),
        P(None, "dp", "tensor"),
        P("tensor", "dp"),
        P(None, "dp", "tensor"),
        P("tensor", "dp"),
        P(),
    )
    return jax.shard_map(
        local,
        mesh=mesh,
        in_specs=placed,
        out_specs=(
            P(("dp", "tensor"), None),
            P(("dp", "tensor"), None),
            P(None, "dp", "tensor"),
            P(None, "dp", "tensor"),
            P(None, "dp", "tensor"),
            P(None, "dp", "tensor"),
            P("tensor", "dp"),
            P("tensor", "dp"),
            P("tensor", "dp"),
            P("tensor", "dp"),
            P(None, "dp", "tensor"),
            P(None, "dp", "tensor"),
            P(None, "dp", "tensor"),
            P(None, "dp", "tensor"),
            P("tensor", "dp"),
            P("tensor", "dp"),
            P("tensor", "dp"),
            P("tensor", "dp"),
            P(),
            P(),
            P(),
            P(),
        ),
        check_vma=False,
    )
```
